256 devices in a mesh: set: 8 (over x, y_lo), dp: 32 (over z, y_hi, core).
Axes of the slice: x: 4, y: 4 (y_hi: 2, y_lo: 2; y = y_hi * 2 + y_lo), z: 8, core: 2. Of those that a mesh axis runs over, the one named last changes fastest.
Arguments:
- embeddings: bfloat16 [16, 4096, 1024], P('set', 'dp'), may hold values from -0.75 to 0.75
- cotangent: bfloat16 [4096, 8192], P('dp', 'set'), may hold values from -0.625 to 0.625
- first_weight: bfloat16 [1920, 8192], P('set'), may hold values from -0.5 to 0.5
- feature_rows: int32 [4096, 16], P('dp'), may hold values from 0 to 16383, as said below
Outputs:
- weight_grad: bfloat16 [1920, 8192], P('set', 'dp')
- table_grad: float32 [16384, 1024], P('dp', 'set')
The draws below stay inside these ranges and needn't reach their ends.
Inputs may be any that keep to these rules, and one draw needn't show every extreme that they name: `feature_rows`: row r is kept by owner r // 512. Among the 2048 ids of each aligned block of 128 samples, one owner, the same for all blocks, holds exactly 128, and every other owner holds as many as any other, up to one.
All inputs are finite; a program needn't handle non-finite values.
Results may differ from the reference program's by a relative error of at most 0.0075.
Values may be sent and summed in bfloat16 or wider, within the bound.
A program may use at most 64 MiB of HBM per device.

```python
import jax
import jax.numpy as jnp
import numpy as np
from jax import lax

K = 64
HID = 8192
F = 16
ROWS_DEV = 512
PAIRS = 120
SETS = 16
GROUP = 128
BATCH = 4096
ROWS = 16384
CAP = 128


def draw_feature_rows(key, part):
    key = jax.random.fold_in(key, 11)
    owner_count = ROWS // ROWS_DEV
    block_count = BATCH // GROUP
    item_count = GROUP * F
    hot_owner = jax.random.randint(jax.random.fold_in(key, 1), (), 0, owner_count)
    position = jnp.arange(item_count)
    baseline = jnp.where(position < CAP, hot_owner, (hot_owner + 1 + (position - CAP) % (owner_count - 1)) % owner_count)
    block_keys = jax.random.split(jax.random.fold_in(key, 2), block_count)
    owner_grid = jax.vmap(lambda block_key: jax.random.permutation(block_key, baseline))(block_keys)
    local_rows = jax.random.randint(jax.random.fold_in(key, 3), (block_count, item_count), 0, ROWS_DEV)
    return (owner_grid * ROWS_DEV + local_rows).reshape(BATCH, F).astype(jnp.int32)


def raised(drawn, stream_key, source, target, parts, factor):
    def block_of(axis_at):
        return (jnp.arange(drawn.shape[axis_at]) // (drawn.shape[axis_at] // parts)).reshape((-1,) + (1,) * (drawn.ndim - 1 - axis_at))

    near = jax.random.permutation(stream_key, parts)[block_of(target)]
    other_side = (block_of(target) + parts // 2) % parts
    return jnp.where((block_of(source) == near) | (block_of(source) == other_side), factor * drawn, drawn)


def level_of(own_key, dims, cuts, low, top_value):
    level = 1.0
    for axis_at, parts in cuts:
        draws = jax.random.uniform(jax.random.fold_in(jax.random.fold_in(own_key, 6), axis_at), (parts,), jnp.float32, low / len(cuts), top_value / len(cuts))
        level = level * jnp.repeat(jnp.exp(draws), dims[axis_at] // parts).reshape((-1,) + (1,) * (len(dims) - 1 - axis_at))
    return level


def gaussian(rng, dims, deviation, bound, cuts=(), kind=jnp.bfloat16):
    result = jax.random.normal(rng, dims, jnp.float32) * deviation
    if len(cuts) > 0:
        result = level_of(rng, dims, cuts, -0.22, 0.18) * result
    return jnp.clip(result, min=-bound, max=bound).astype(kind)


def noise_with(key, extent, deviation, limit, pieces, heavy, kind=jnp.bfloat16):
    values = deviation * jax.random.normal(key, extent, jnp.float32)
    if pieces:
        values = values * level_of(key, extent, pieces, -0.22, 0.18)
    return jnp.clip(raised(values, jax.random.fold_in(key, 3), *heavy), -limit, limit).astype(kind)


def setup_inputs(seed: int = 0) -> dict:
    arg_keys = jax.random.split(jax.random.key(seed), 5)
    return {
        "embeddings": gaussian(arg_keys[0], (SETS, BATCH, F * K), 0.125, 0.75, ((0, 8), (1, 32))),
        "cotangent": noise_with(arg_keys[1], (BATCH, HID), 0.05, 0.625, ((0, 32), (1, 8)), (0, 1, 32, 2.75)),
        "first_weight": gaussian(arg_keys[2], (SETS * PAIRS, HID), PAIRS ** -0.5, 0.5, ((0, 8),)),
        "feature_rows": draw_feature_rows(jax.random.fold_in(arg_keys[4], 71), 0),
    }


def pair_table(width):
    first_feature, second_feature = np.triu_indices(width, 1)
    flat_pairs = first_feature * width + second_feature
    table_np = (np.arange(width * width)[:, None] == flat_pairs[None, :]).astype(np.float32)
    return jnp.asarray(table_np)


def reference(embeddings, cotangent, first_weight, feature_rows):
    selector = pair_table(F)
    sets_total = embeddings.shape[0]
    batch_rows = embeddings.shape[1]
    pair_count = selector.shape[1]
    weight_sets = first_weight.reshape(sets_total, pair_count, HID)
    flat_rows = feature_rows.reshape(-1).astype(jnp.int32)
    spread_table = selector.T.astype(jnp.bfloat16)

    def per_set(operands):
        embedded_raw, weight_block = operands
        embedded = embedded_raw.reshape(batch_rows, F, K).astype(jnp.float32)
        gram_flat = jnp.einsum("bfk,bgk->bfg", embedded, embedded).reshape(batch_rows, F * F)
        pairs = jnp.dot(gram_flat, selector, precision=lax.Precision.HIGHEST).astype(jnp.bfloat16)
        weight_part = jnp.dot(pairs.T, cotangent, preferred_element_type=jnp.float32).astype(jnp.bfloat16)
        pair_grad = jnp.dot(cotangent, weight_block.T, preferred_element_type=jnp.float32).astype(jnp.bfloat16)
        spread = jnp.dot(pair_grad, spread_table, preferred_element_type=jnp.float32).reshape(batch_rows, F, F)
        symmetric = spread + jnp.swapaxes(spread, 1, 2)
        emb_grad = jnp.einsum("bfg,bgk->bfk", symmetric, embedded).astype(jnp.bfloat16)
        table_part = jnp.zeros((ROWS, K), jnp.float32).at[flat_rows].add(emb_grad.reshape(-1, K).astype(jnp.float32))
        return weight_part, table_part

    weight_parts, table_parts = lax.map(per_set, (embeddings, weight_sets))
    weight_grad = weight_parts.reshape(sets_total * pair_count, HID)
    table_grad = jnp.transpose(table_parts, (1, 0, 2)).reshape(ROWS, sets_total * K)
    return weight_grad, table_grad
```

```python
import functools

import jax
import jax.numpy as jnp
import numpy as np
from jax import lax
from jax.experimental import pallas as pl
from jax.experimental.pallas import tpu as pltpu
from jax.sharding import PartitionSpec as P

K = 64
F = 16
ROWS_DEV = 512
PAIRS = 120
B = 128
KEEP = 62
XROWS = 80
DP = 32
BF = jnp.bfloat16
F32 = jnp.float32
MESH = pl.DeviceIdType.MESH


def constants():
    first, second = np.triu_indices(F, 1)
    spread = np.zeros((256, F, 16), np.float32)
    mask = np.zeros((F, 16, 256), np.float32)
    for p in range(PAIRS):
        spread[p, second[p], :] = 1
        spread[128 + p, first[p], :] = 1
        mask[first[p], :, p] = 1
        mask[second[p], :, 128 + p] = 1
    spread = spread.reshape(256, 256)
    pick = np.ascontiguousarray(spread[:128].T)
    return [a.astype(BF) for a in (spread, pick, mask.reshape(256, 256))]


def dot(a, b):
    return jnp.dot(a, b, preferred_element_type=F32)


def dot_nt(a, b):
    return lax.dot_general(a, b, (((1,), (1,)), ((), ())), preferred_element_type=F32)


def kernel(emb_ref, cot_ref, w_ref, rows_ref, spread_ref, pick_ref, mask_ref, wg_ref, tg_ref,
           cot_v, sib_v, w_v, ei, items, pairs_v, pt_v, pg_v, rowpad, pos_v, vals_v, meta_v,
           hot_v, hotx_v, rs_s, rs_r, y_s, y_r, send_v, recv_v, x_s, x_r,
           loc_sem, ag_ss, ag_rs, sib_ss, sib_rs, pt_ss, pt_rs, rs_ss, rs_rs, y_ss, y_rs,
           a_ss, a_rs, x_ss, x_rs):
    me_s = lax.axis_index("set")
    me_d = lax.axis_index("dp")
    x, yl = me_s // 2, me_s % 2
    right = ((x + 1) % 4) * 2 + yl
    left = ((x + 3) % 4) * 2 + yl
    opp = ((x + 2) % 4) * 2 + yl
    over = me_s + 1 - 2 * yl
    right_o = right + 1 - 2 * yl
    left_o = left + 1 - 2 * yl
    opp_o = opp + 1 - 2 * yl
    z, yh, core = me_d // 4, (me_d // 2) % 2, me_d % 2
    twin = me_d + 1 - 2 * core
    y_part = me_d + 2 - 4 * yh
    z_up, z_down = (me_d + 4) % DP, (me_d + 28) % DP

    def rcopy(src, dst, ss, rs, **where):
        return pltpu.make_async_remote_copy(
            src_ref=src, dst_ref=dst, send_sem=ss, recv_sem=rs, device_id=where, device_id_type=MESH)

    own_copies = []
    for h in range(2):
        for cc in range(2):
            own_copies.append(pltpu.make_async_copy(
                cot_ref.at[:, pl.ds((h * 2 + cc) * 256, 256)], cot_v.at[me_s, cc, h], loc_sem.at[h * 2 + cc]))
    w_copy = pltpu.make_async_copy(w_ref, w_v, loc_sem.at[4])
    for copy in own_copies:
        copy.start()
    w_copy.start()

    barrier = pltpu.get_barrier_semaphore()
    for peer in (right, left, over):
        pl.semaphore_signal(barrier, inc=1, device_id={"set": peer}, device_id_type=MESH)

    def greet(i, carry):
        pl.semaphore_signal(barrier, inc=1, device_id={"dp": (me_d + i) % DP}, device_id_type=MESH)
        return carry

    lax.fori_loop(1, DP, greet, 0)
    for copy in own_copies:
        copy.wait()
    pl.semaphore_wait(barrier, 3 + DP - 1)

    def ag(k, src, peer):
        return rcopy(src, src, ag_ss.at[k], ag_rs.at[k], set=peer)

    def ag_wait(k, block):
        rcopy(block, block, ag_ss.at[k], ag_rs.at[k], set=right).wait_recv()

    sent = []

    def start(copy):
        copy.start()
        sent.append(copy)

    start(ag(0, cot_v.at[me_s], right))
    start(ag(1, cot_v.at[me_s], left))
    start(ag(2, cot_v.at[me_s], over))

    def to_twin(t, j):
        start(rcopy(cot_v.at[j, 1 - core], sib_v.at[j], sib_ss.at[t], sib_rs.at[t], dp=twin))

    to_twin(0, me_s)

    lane = lax.broadcasted_iota(jnp.int32, (B, 128), 1)
    for m in range(8):
        a = emb_ref[0, :, m * 128:(m + 1) * 128].astype(F32)
        b = emb_ref[1, :, m * 128:(m + 1) * 128].astype(F32)
        ei[2 * m] = jnp.where(lane < 64, a, pltpu.roll(b, 64, 1)).astype(BF)
        ei[2 * m + 1] = jnp.where(lane < 64, pltpu.roll(a, 64, 1), b).astype(BF)

    def diagonal():
        r = lax.broadcasted_iota(jnp.int32, (256, 256), 0)
        c = lax.broadcasted_iota(jnp.int32, (256, 256), 1)
        return (r % 16) == (c % 16)

    def group_rows(g):
        return pl.ds(pl.multiple_of(g * 16, 16), 16)

    def pair_step(g, carry):
        eg = ei[:, group_rows(g), :].reshape(256, 128)
        lane_g = lax.broadcasted_iota(jnp.int32, (256, 128), 1)
        for s in range(2):
            half = jnp.where((lane_g < 64) == (s == 0), eg.astype(F32), 0.0).astype(BF)
            gram = jnp.where(diagonal(), dot_nt(half, eg), 0.0).astype(BF)
            picked = dot(gram, pick_ref[...]) * mask_ref[:, :128].astype(F32)
            pairs_v[group_rows(g), s * 128:(s + 1) * 128] = jnp.sum(picked.reshape(F, 16, 128), axis=0)
        return carry

    lax.fori_loop(0, B // 16, pair_step, 0)
    turned = pairs_v[...].T
    pt_v[:, :B] = jnp.concatenate([turned[:PAIRS], turned[128:128 + PAIRS]], axis=0).astype(BF)
    start(rcopy(pt_v.at[:, pl.ds(0, B)], pt_v.at[:, pl.ds(B, B)], pt_ss, pt_rs, dp=twin))

    w_copy.wait()
    pg_v[...] = jnp.zeros_like(pg_v)

    def pg_add(j):
        total = None
        for h in range(2):
            for cc in range(2):
                cols = pl.ds(pl.multiple_of(j * 1024 + (h * 2 + cc) * 256, 256), 256)
                part = dot_nt(cot_v[j, cc, h], w_v[:, cols])
                total = part if total is None else total + part
        pg_v[:, :2 * PAIRS] += total

    pg_add(me_s)

    rowpad[...] = jnp.zeros_like(rowpad)
    rowpad[:, :F] = rows_ref[...].astype(F32)
    rows_t = rowpad[...].T[:F]
    owner = jnp.floor(rows_t * (1.0 / ROWS_DEV))
    local = rows_t - owner * ROWS_DEV
    local_hi = jnp.floor(local * (1.0 / 256))
    g_hi = jnp.floor(rows_t * (1.0 / 128))
    before = (lax.broadcasted_iota(jnp.int32, (128, 128), 0)
              < lax.broadcasted_iota(jnp.int32, (128, 128), 1)).astype(F32).astype(BF)
    owner_id = lax.broadcasted_iota(jnp.int32, (DP, 128), 0).astype(F32)
    seen = jnp.zeros((DP, 1), F32)
    vals_v[...] = jnp.zeros_like(vals_v)
    for f in range(F):
        hot = jnp.where(owner_id == owner[f:f + 1], 1.0, 0.0)
        earlier = dot(hot.astype(BF), before) + seen
        seen = seen + jnp.sum(hot, axis=1, keepdims=True)
        rank = jnp.sum(hot * earlier, axis=0, keepdims=True)
        pos = jnp.where(rank < KEEP, owner[f:f + 1] * 64 + rank, DP * 64 + rank - KEEP)
        pos_v[f:f + 1, :] = pos.astype(jnp.int32)
        cols = slice(f * 128, (f + 1) * 128)
        vals_v[0:1, cols] = local[f:f + 1] - 256 * local_hi[f:f + 1]
        vals_v[1:2, cols] = local_hi[f:f + 1]
        vals_v[2:3, cols] = rows_t[f:f + 1] - 128 * g_hi[f:f + 1]
        vals_v[3:4, cols] = g_hi[f:f + 1]

    def hot_step(k, carry):
        slot = lax.broadcasted_iota(jnp.int32, (256, 128), 0) + k * 256
        for f in range(F):
            hot_v[k, :, f * 128:(f + 1) * 128] = jnp.where(slot == pos_v[f:f + 1, :], 1.0, 0.0).astype(BF)
        ids = dot_nt(vals_v[...].astype(BF), hot_v[k])
        low = lax.broadcasted_iota(jnp.int32, (1, 128), 1) < 64
        for q in range(4):
            cols = slice((q // 2) * 128, (q // 2) * 128 + 128)
            lo, hi = ids[0:1, cols], ids[1:2, cols]
            if q % 2 == 0:
                row = jnp.where(low, lo, pltpu.roll(jnp.broadcast_to(hi, (8, 128)), 64, 1)[0:1])
            else:
                row = jnp.where(low, pltpu.roll(jnp.broadcast_to(lo, (8, 128)), 64, 1)[0:1], hi)
            meta_v[k, q:q + 1, :] = row
        return carry

    ag_wait(0, cot_v.at[left])
    start(ag(5, cot_v.at[left, 0], right))
    ag_wait(1, cot_v.at[right])
    start(ag(6, cot_v.at[right, 1], left))
    ag_wait(2, cot_v.at[over])
    start(ag(3, cot_v.at[over], right))
    start(ag(4, cot_v.at[over], left))
    to_twin(1, left)
    to_twin(2, right)
    to_twin(3, over)
    pg_add(left)
    pg_add(right)
    pg_add(over)
    lax.fori_loop(0, 4, hot_step, 0)

    ag_wait(5, cot_v.at[opp, 0])
    start(ag(7, cot_v.at[opp, 0], over))
    ag_wait(6, cot_v.at[opp, 1])
    start(ag(8, cot_v.at[opp, 1], over))
    to_twin(4, opp)
    pg_add(opp)
    lax.fori_loop(4, 8, hot_step, 0)
    slot_x = lax.broadcasted_iota(jnp.int32, (XROWS, 128), 0) + DP * 64
    for f in range(F):
        hotx_v[:, f * 128:(f + 1) * 128] = jnp.where(slot_x == pos_v[f:f + 1, :], 1.0, 0.0).astype(BF)
    ids_x = dot_nt(vals_v[...].astype(BF), hotx_v[...])

    ag_wait(3, cot_v.at[left_o])
    ag_wait(4, cot_v.at[right_o])
    to_twin(5, left_o)
    to_twin(6, right_o)
    pg_add(left_o)
    pg_add(right_o)
    ag_wait(7, cot_v.at[opp_o, 0])
    ag_wait(8, cot_v.at[opp_o, 1])
    to_twin(7, opp_o)
    pg_add(opp_o)

    rcopy(pt_v.at[:, pl.ds(0, B)], pt_v.at[:, pl.ds(B, B)], pt_ss, pt_rs, dp=twin).wait_recv()
    for t, j in enumerate((me_s, left, right, over, opp, left_o, right_o, opp_o)):
        rcopy(cot_v.at[j, 1 - core], sib_v.at[j], sib_ss.at[t], sib_rs.at[t], dp=twin).wait_recv()

    def part(j, h):
        return dot(pt_v[...], jnp.concatenate([cot_v[j, core, h], sib_v[j, h]], axis=0))

    def rs_copy(way, k, h):
        return rcopy(rs_s.at[way, k, h], rs_r.at[way, k, h], rs_ss.at[way, k, h], rs_rs.at[way, k, h],
                     dp=z_up if way else z_down)

    def rs_step(way, k, h):
        j = (z + 12 - k) % 8 if way else (z + 4 + k) % 8
        value = part(j, h)
        if k >= 2 or (k == 1 and h == way):
            rs_copy(way, k - 1, h).wait_recv()
            value = value + rs_r[way, k - 1, h].astype(F32)
        rs_s[way, k, h] = value.astype(BF)
        start(rs_copy(way, k, h))

    rs_step(0, 0, 0)
    rs_step(1, 0, 1)
    rs_step(0, 1, 1)
    rs_step(1, 1, 0)

    pg_all = pg_v[...]
    pg_v[...] = pg_all.astype(BF).astype(F32)

    def emb_step(g, carry):
        eg = ei[:, group_rows(g), :].reshape(256, 128)
        a = pg_v[group_rows(g), :]
        grads = []
        for s in range(2):
            one = (a if s == 0 else pltpu.roll(a, 256 - PAIRS, 1))[:, :128]
            both = jnp.concatenate([one, one], axis=1).astype(BF)
            tall = jnp.concatenate([both] * F, axis=0) * mask_ref[...]
            sym = jnp.where(diagonal(), dot(tall, spread_ref[...]), 0.0).astype(BF)
            grads.append(dot(sym, eg))
        lane_g = lax.broadcasted_iota(jnp.int32, (256, 128), 1)
        items[:, group_rows(g), :] = jnp.where(lane_g < 64, grads[0], grads[1]).astype(BF).reshape(F, 16, 128)
        return carry

    lax.fori_loop(0, B // 16, emb_step, 0)

    rs_step(0, 1, 0)
    rs_step(1, 1, 1)

    def x_copy(i):
        return rcopy(x_s, x_r.at[me_d], x_ss.at[i], x_rs.at[me_d], dp=(me_d + i) % DP)

    x_tile = dot(hotx_v[...], items[...].reshape(B * F, 128))
    row_x = lax.broadcasted_iota(jnp.int32, (XROWS, 128), 0)
    ids_x = jnp.concatenate([ids_x, jnp.zeros((ids_x.shape[0], 128 - XROWS), F32)], axis=1)
    x_tile = jnp.where(row_x == 66, ids_x[2:3], jnp.where(row_x == 67, ids_x[3:4], x_tile))
    x_s[...] = x_tile.astype(BF)
    x_r[me_d] = x_tile.astype(BF)

    def x_start(i, carry):
        x_copy(i).start()
        return carry

    lax.fori_loop(1, DP, x_start, 0)

    def a_copy(o):
        return rcopy(send_v.at[o], recv_v.at[me_d], a_ss.at[o], a_rs.at[me_d], dp=o)

    def a_step(i, carry):
        k = (z + 4 + i) % 8
        tile = dot(hot_v[k], items[...].reshape(B * F, 128))
        row = lax.broadcasted_iota(jnp.int32, (64, 128), 0)
        for q in range(4):
            o = k * 4 + q
            block = jnp.where(row == KEEP, meta_v[k, q:q + 1, :], tile[q * 64:(q + 1) * 64]).astype(BF)
            send_v[o] = block

            @pl.when(o == me_d)
            def _():
                recv_v[o] = block

            @pl.when(o != me_d)
            def _():
                a_copy(o).start()
        return carry

    lax.fori_loop(0, 4, a_step, 0)
    for way in range(2):
        rs_step(way, 2, 0)
        rs_step(way, 2, 1)
    lax.fori_loop(4, 8, a_step, 0)
    for way in range(2):
        rs_step(way, 3, 0)
        rs_step(way, 3, 1)

    tg_ref[...] = jnp.zeros_like(tg_ref)
    row_id = lax.broadcasted_iota(jnp.int32, (ROWS_DEV, 128), 0).astype(F32)

    def a_add(i, carry):
        k = (z + 8 - i) % 8
        low = lax.broadcasted_iota(jnp.int32, (8, 128), 1) < 64
        dead = lax.broadcasted_iota(jnp.int32, (8, 128), 1) % 64 >= KEEP
        for q in range(4):
            @pl.when(k * 4 + q != me_d)
            def _():
                rcopy(send_v.at[me_d], recv_v.at[k * 4 + q], a_ss.at[me_d], a_rs.at[k * 4 + q], dp=twin).wait_recv()
        ids = []
        for q in range(4):
            got = jnp.broadcast_to(recv_v[k * 4 + q, KEEP:KEEP + 1, :].astype(F32), (8, 128))
            turn = pltpu.roll(got, 64, 1)
            ids.append(got + 256 * turn if q % 2 == 0 else turn + 256 * got)
        hots = []
        for m in range(2):
            both = jnp.where(dead, -1.0, jnp.where(low, ids[2 * m], ids[2 * m + 1]))[0:1]
            hots.append(jnp.where(row_id == both, 1.0, 0.0).astype(BF))
        values = recv_v[pl.ds(pl.multiple_of(k * 4, 4), 4)].reshape(256, 128)
        tg_ref[...] += dot(jnp.concatenate(hots, axis=1), values)
        return carry

    lax.fori_loop(0, 8, a_add, 0)

    for way in range(2):
        for h in range(2):
            rs_copy(way, 3, h).wait_recv()

    def whole(h):
        return part(z, h) + rs_r[0, 3, h].astype(F32) + rs_r[1, 3, h].astype(F32)

    y_s[...] = whole(1 - yh).astype(BF)
    y_copy = rcopy(y_s, y_r, y_ss, y_rs, dp=y_part)
    y_copy.start()

    base = (me_d * ROWS_DEV).astype(F32)

    def x_add(i, carry):
        src = (me_d + i) % DP

        @pl.when(src != me_d)
        def _():
            rcopy(x_s, x_r.at[src], x_ss.at[0], x_rs.at[src], dp=twin).wait_recv()

        low = x_r[src, 66:67, :].astype(F32)
        high = x_r[src, 67:68, :].astype(F32)
        ids = low + 128 * high - base
        ids = jnp.where(lax.broadcasted_iota(jnp.int32, (1, 128), 1) < 66, ids, -1.0)
        hot = jnp.where(row_id == ids, 1.0, 0.0).astype(BF)
        tg_ref[...] += dot(hot[:, :XROWS], x_r[src])
        return carry

    lax.fori_loop(0, DP, x_add, 0)

    last = whole(yh)
    y_copy.wait()
    wg_ref[...] = (last + y_r[...].astype(F32)).astype(BF)

    for copy in sent:
        copy.wait_send()

    def drain(i, carry):
        x_copy(i).wait_send()
        a_copy((me_d + i) % DP).wait_send()
        return carry

    lax.fori_loop(1, DP, drain, 0)


def on_device(embeddings, cotangent, first_weight, feature_rows):
    vmem = pl.BlockSpec(memory_space=pltpu.VMEM)
    hbm = pl.BlockSpec(memory_space=pl.ANY)
    dma = pltpu.SemaphoreType.DMA
    consts = [jnp.asarray(a) for a in constants()]
    return pl.pallas_call(
        kernel,
        out_shape=(jax.ShapeDtypeStruct((2 * PAIRS, 256), BF), jax.ShapeDtypeStruct((ROWS_DEV, 128), F32)),
        in_specs=[vmem, hbm, hbm, vmem, vmem, vmem, vmem],
        out_specs=(vmem, vmem),
        scratch_shapes=[
            pltpu.VMEM((8, 2, 2, B, 256), BF),
            pltpu.VMEM((8, 2, B, 256), BF),
            pltpu.VMEM((2 * PAIRS, 8192), BF),
            pltpu.VMEM((F, B, 128), BF),
            pltpu.VMEM((F, B, 128), BF),
            pltpu.VMEM((B, 256), F32),
            pltpu.VMEM((2 * PAIRS, 256), BF),
            pltpu.VMEM((B, 256), F32),
            pltpu.VMEM((B, 128), F32),
            pltpu.VMEM((F, 128), jnp.int32),
            pltpu.VMEM((16, B * F), F32),
            pltpu.VMEM((8, 8, 128), F32),
            pltpu.VMEM((8, 256, B * F), BF),
            pltpu.VMEM((XROWS, B * F), BF),
            pltpu.VMEM((2, 4, 2, 2 * PAIRS, 256), BF),
            pltpu.VMEM((2, 4, 2, 2 * PAIRS, 256), BF),
            pltpu.VMEM((2 * PAIRS, 256), BF),
            pltpu.VMEM((2 * PAIRS, 256), BF),
            pltpu.VMEM((DP, 64, 128), BF),
            pltpu.VMEM((DP, 64, 128), BF),
            pltpu.VMEM((XROWS, 128), BF),
            pltpu.VMEM((DP, XROWS, 128), BF),
            dma((5,)), dma((9,)), dma((9,)), dma((8,)), dma((8,)), dma, dma,
            dma((2, 4, 2)), dma((2, 4, 2)), dma, dma,
            dma((DP,)), dma((DP,)), dma((DP,)), dma((DP,)),
        ],
        compiler_params=pltpu.CompilerParams(
            collective_id=0, has_side_effects=True, vmem_limit_bytes=56 * 1024 * 1024),
    )(embeddings, cotangent, first_weight, feature_rows, *consts)


def solution(mesh):
    return jax.shard_map(
        on_device,
        mesh=mesh,
        in_specs=(P("set", "dp", None), P("dp", "set"), P("set", None), P("dp", None)),
        out_specs=(P("set", "dp"), P("dp", "set")),
        check_vma=False,
    )
```

```python
import functools

import jax
import jax.numpy as jnp
import numpy as np
from jax import lax
from jax.experimental import pallas as pl
from jax.experimental.pallas import tpu as pltpu
from jax.sharding import PartitionSpec as P

K = 64
F = 16
ROWS_DEV = 512
PAIRS = 120
B = 128
KEEP = 62
XROWS = 80
DP = 32
BF = jnp.bfloat16
F32 = jnp.float32
MESH = pl.DeviceIdType.MESH


def constants():
    first, second = np.triu_indices(F, 1)
    spread = np.zeros((256, F, 16), np.float32)
    mask = np.zeros((F, 16, 256), np.float32)
    for p in range(PAIRS):
        spread[p, second[p], :] = 1
        spread[128 + p, first[p], :] = 1
        mask[first[p], :, p] = 1
        mask[second[p], :, 128 + p] = 1
    spread = spread.reshape(256, 256)
    pick = np.ascontiguousarray(spread[:128].T)
    return [a.astype(BF) for a in (spread, pick, mask.reshape(256, 256))]


def dot(a, b):
    return jnp.dot(a, b, preferred_element_type=F32)


def dot_nt(a, b):
    return lax.dot_general(a, b, (((1,), (1,)), ((), ())), preferred_element_type=F32)


def kernel(emb_hbm, cot_ref, w_ref, rows_ref, spread_hbm, pick_hbm, mask_hbm, wg_ref, tg_ref,
           emb_ref, spread_ref, pick_ref, mask_ref,
           cot_v, sib_v, w_v, ei, items, pairs_v, pt_v, pg_v, pos_v, vals_v, meta_v,
           hot_v, hotx_v, rs_s, rs_r, y_s, y_r, send_v, recv_v, x_v,
           loc_sem, ag_ss, ag_rs, sib_ss, sib_rs, pt_ss, pt_rs, rs_ss, rs_rs, y_ss, y_rs,
           a_ss, a_rs, x_ss, x_rs):
    me_s = lax.axis_index("set")
    me_d = lax.axis_index("dp")
    x, yl = me_s // 2, me_s % 2
    right = ((x + 1) % 4) * 2 + yl
    left = ((x + 3) % 4) * 2 + yl
    opp = ((x + 2) % 4) * 2 + yl
    over = me_s + 1 - 2 * yl
    right_o = right + 1 - 2 * yl
    left_o = left + 1 - 2 * yl
    opp_o = opp + 1 - 2 * yl
    z, yh, core = me_d // 4, (me_d // 2) % 2, me_d % 2
    twin = me_d + 1 - 2 * core
    y_part = me_d + 2 - 4 * yh
    z_up, z_down = (me_d + 4) % DP, (me_d + 28) % DP

    def rcopy(src, dst, ss, rs, **where):
        return pltpu.make_async_remote_copy(
            src_ref=src, dst_ref=dst, send_sem=ss, recv_sem=rs, device_id=where, device_id_type=MESH)

    own_copies = []
    for h in range(2):
        for cc in range(2):
            own_copies.append(pltpu.make_async_copy(
                cot_ref.at[:, pl.ds((h * 2 + cc) * 256, 256)], cot_v.at[me_s, cc, h], loc_sem.at[h * 2 + cc]))
    inputs = ((emb_hbm, emb_ref), (pick_hbm, pick_ref), (mask_hbm, mask_ref), (spread_hbm, spread_ref), (w_ref, w_v))
    in_copies = [pltpu.make_async_copy(a, b, loc_sem.at[4 + i]) for i, (a, b) in enumerate(inputs)]
    for copy in own_copies + in_copies:
        copy.start()

    barrier = pltpu.get_barrier_semaphore()
    for peer in (right, left, over):
        pl.semaphore_signal(barrier, inc=1, device_id={"set": peer}, device_id_type=MESH)

    def greet(i, carry):
        pl.semaphore_signal(barrier, inc=1, device_id={"dp": (me_d + i) % DP}, device_id_type=MESH)
        return carry

    lax.fori_loop(1, DP, greet, 0)
    for copy in own_copies:
        copy.wait()
    pl.semaphore_wait(barrier, 3 + DP - 1)

    sent = []

    def start(copy):
        copy.start()
        sent.append(copy)

    def ag(k, src, peer):
        start(rcopy(src, src, ag_ss.at[k], ag_rs.at[k], set=peer))

    def ag_wait(k, block):
        rcopy(block, block, ag_ss.at[k], ag_rs.at[k], set=right).wait_recv()

    ag(0, cot_v.at[me_s, 0], right)
    ag(2, cot_v.at[me_s, 1], left)
    ag(4, cot_v.at[me_s], over)
    ag(1, cot_v.at[me_s, 1], right)
    ag(3, cot_v.at[me_s, 0], left)

    def twin_copy(t, j):
        return rcopy(cot_v.at[j, 1 - core], sib_v.at[j], sib_ss.at[t], sib_rs.at[t], dp=twin)

    def to_twin(t, j):
        start(twin_copy(t, j))

    to_twin(0, me_s)

    for copy in in_copies[:4]:
        copy.wait()
    lane = lax.broadcasted_iota(jnp.int32, (B, 128), 1)
    for m in range(8):
        a = emb_ref[0, :, m * 128:(m + 1) * 128].astype(F32)
        b = emb_ref[1, :, m * 128:(m + 1) * 128].astype(F32)
        ei[2 * m] = jnp.where(lane < 64, a, pltpu.roll(b, 64, 1)).astype(BF)
        ei[2 * m + 1] = jnp.where(lane < 64, pltpu.roll(a, 64, 1), b).astype(BF)

    def diagonal():
        r = lax.broadcasted_iota(jnp.int32, (256, 256), 0)
        c = lax.broadcasted_iota(jnp.int32, (256, 256), 1)
        return (r % 16) == (c % 16)

    def group_rows(g):
        return pl.ds(pl.multiple_of(g * 16, 16), 16)

    def pair_step(g, carry):
        eg = ei[:, group_rows(g), :].reshape(256, 128)
        lane_g = lax.broadcasted_iota(jnp.int32, (256, 128), 1)
        for s in range(2):
            half = jnp.where((lane_g < 64) == (s == 0), eg.astype(F32), 0.0).astype(BF)
            gram = jnp.where(diagonal(), dot_nt(half, eg), 0.0).astype(BF)
            picked = dot(gram, pick_ref[...]) * mask_ref[:, :128].astype(F32)
            pairs_v[group_rows(g), s * 128:(s + 1) * 128] = jnp.sum(picked.reshape(F, 16, 128), axis=0)
        return carry

    lax.fori_loop(0, 4, pair_step, 0)

    ag_wait(0, cot_v.at[left, 0])
    ag(5, cot_v.at[left, 0], right)
    ag_wait(2, cot_v.at[right, 1])
    ag(6, cot_v.at[right, 1], left)

    lax.fori_loop(4, 8, pair_step, 0)
    turned = pairs_v[...].T
    pt_v[:, :B] = jnp.concatenate([turned[:PAIRS], turned[128:128 + PAIRS]], axis=0).astype(BF)
    pt_copy = rcopy(pt_v.at[:, pl.ds(0, B)], pt_v.at[:, pl.ds(B, B)], pt_ss, pt_rs, dp=twin)
    start(pt_copy)

    ag_wait(4, cot_v.at[over])
    ag(7, cot_v.at[over], right)
    ag(8, cot_v.at[over], left)
    to_twin(1, over)
    ag_wait(1, cot_v.at[left, 1])
    ag_wait(3, cot_v.at[right, 0])
    to_twin(2, left)
    to_twin(3, right)

    in_copies[4].wait()
    pg_v[...] = jnp.zeros_like(pg_v)

    def pg_add(j):
        total = None
        for h in range(2):
            for cc in range(2):
                cols = pl.ds(pl.multiple_of(j * 1024 + (h * 2 + cc) * 256, 256), 256)
                term = dot_nt(cot_v[j, cc, h], w_v[:, cols])
                total = term if total is None else total + term
        pg_v[:, :2 * PAIRS] += total

    def part(j, h):
        return dot(pt_v[...], jnp.concatenate([cot_v[j, core, h], sib_v[j, h]], axis=0))

    def rs_copy(way, k, h):
        return rcopy(rs_s.at[way, k, h], rs_r.at[way, k, h], rs_ss.at[way, k, h], rs_rs.at[way, k, h],
                     dp=z_up if way else z_down)

    def rs_step(late, way, k, h):
        j = (z + 12 - k) % 8 if way else (z + 4 + k) % 8
        is_late = (j == left_o) | (j == right_o) | (j == opp_o)

        @pl.when(is_late if late else jnp.logical_not(is_late))
        def _():
            value = part(j, h)
            if k >= 2 or (k == 1 and h == way):
                rs_copy(way, k - 1, h).wait_recv()
                value = value + rs_r[way, k - 1, h].astype(F32)
            rs_s[way, k, h] = value.astype(BF)
            rs_copy(way, k, h).start()

    def rs_round(late, n):
        for way in range(2):
            if n < 4:
                rs_step(late, way, n, way)
        for way in range(2):
            if n < 3:
                rs_step(late, way, n + 1, 1 - way)

    for j in (me_s, over, left, right):
        pg_add(j)

    ag_wait(5, cot_v.at[opp, 0])
    ag(9, cot_v.at[opp, 0], over)
    ag_wait(6, cot_v.at[opp, 1])
    ag(10, cot_v.at[opp, 1], over)
    to_twin(4, opp)

    rows_t = rows_ref[...].astype(F32)
    owner = jnp.floor(rows_t * (1.0 / ROWS_DEV))
    local = rows_t - owner * ROWS_DEV
    local_hi = jnp.floor(local * (1.0 / 256))
    g_hi = jnp.floor(rows_t * (1.0 / 128))
    before = (lax.broadcasted_iota(jnp.int32, (128, 128), 0)
              < lax.broadcasted_iota(jnp.int32, (128, 128), 1)).astype(F32).astype(BF)
    owner_id = lax.broadcasted_iota(jnp.int32, (DP, 128), 0).astype(F32)
    seen = jnp.zeros((DP, 1), F32)
    vals_v[...] = jnp.zeros_like(vals_v)
    for f in range(F):
        hot = jnp.where(owner_id == owner[f:f + 1], 1.0, 0.0)
        earlier = dot(hot.astype(BF), before) + seen
        seen = seen + jnp.sum(hot, axis=1, keepdims=True)
        rank = jnp.sum(hot * earlier, axis=0, keepdims=True)
        pos = jnp.where(rank < KEEP, owner[f:f + 1] * 64 + rank, DP * 64 + rank - KEEP)
        pos_v[f:f + 1, :] = pos.astype(jnp.int32)
        cols = slice(f * 128, (f + 1) * 128)
        vals_v[0:1, cols] = local[f:f + 1] - 256 * local_hi[f:f + 1]
        vals_v[1:2, cols] = local_hi[f:f + 1]
        vals_v[2:3, cols] = rows_t[f:f + 1] - 128 * g_hi[f:f + 1]
        vals_v[3:4, cols] = g_hi[f:f + 1]

    def hot_step(k, carry):
        slot = lax.broadcasted_iota(jnp.int32, (256, 128), 0) + k * 256
        for f in range(F):
            hot_v[k, :, f * 128:(f + 1) * 128] = jnp.where(slot == pos_v[f:f + 1, :], 1.0, 0.0).astype(BF)
        ids = dot_nt(vals_v[...].astype(BF), hot_v[k])
        low = lax.broadcasted_iota(jnp.int32, (1, 128), 1) < 64
        for q in range(4):
            cols = slice((q // 2) * 128, (q // 2) * 128 + 128)
            lo, hi = ids[0:1, cols], ids[1:2, cols]
            if q % 2 == 0:
                row = jnp.where(low, lo, pltpu.roll(jnp.broadcast_to(hi, (8, 128)), 64, 1)[0:1])
            else:
                row = jnp.where(low, pltpu.roll(jnp.broadcast_to(lo, (8, 128)), 64, 1)[0:1], hi)
            meta_v[k, q:q + 1, :] = row
        return carry

    pt_copy.wait_recv()
    for t, j in enumerate((me_s, over, left, right, opp)):
        twin_copy(t, j).wait_recv()
    rs_round(False, 0)
    pg_add(opp)
    lax.fori_loop(0, 8, hot_step, 0)
    slot_x = lax.broadcasted_iota(jnp.int32, (XROWS, 128), 0) + DP * 64
    for f in range(F):
        hotx_v[:, f * 128:(f + 1) * 128] = jnp.where(slot_x == pos_v[f:f + 1, :], 1.0, 0.0).astype(BF)
    ids_x = dot_nt(vals_v[...].astype(BF), hotx_v[...])
    x_v[:, :, :, XROWS:] = jnp.zeros((2, 2, 8, 128 - XROWS, 128), BF)
    rs_round(False, 1)

    ag_wait(9, cot_v.at[opp_o, 0])
    ag_wait(10, cot_v.at[opp_o, 1])
    to_twin(5, opp_o)
    pg_add(opp_o)
    ag_wait(7, cot_v.at[left_o])
    to_twin(6, left_o)
    ag_wait(8, cot_v.at[right_o])
    to_twin(7, right_o)
    pg_add(left_o)
    pg_add(right_o)

    pg_all = pg_v[...]
    pg_v[...] = pg_all.astype(BF).astype(F32)

    def emb_step(g, carry):
        eg = ei[:, group_rows(g), :].reshape(256, 128)
        a = pg_v[group_rows(g), :]
        grads = []
        for s in range(2):
            one = (a if s == 0 else pltpu.roll(a, 256 - PAIRS, 1))[:, :128]
            both = jnp.concatenate([one, one], axis=1).astype(BF)
            tall = jnp.concatenate([both] * F, axis=0) * mask_ref[...]
            sym = jnp.where(diagonal(), dot(tall, spread_ref[...]), 0.0).astype(BF)
            grads.append(dot(sym, eg))
        lane_g = lax.broadcasted_iota(jnp.int32, (256, 128), 1)
        items[:, group_rows(g), :] = jnp.where(lane_g < 64, grads[0], grads[1]).astype(BF).reshape(F, 16, 128)
        return carry

    lax.fori_loop(0, 4, emb_step, 0, unroll=2)
    for t, j in enumerate((opp_o, left_o, right_o)):
        twin_copy(5 + t, j).wait_recv()
    rs_round(True, 0)
    rs_round(False, 2)
    lax.fori_loop(4, 8, emb_step, 0, unroll=2)

    x_tile = dot(hotx_v[...], items[...].reshape(B * F, 128))
    row_x = lax.broadcasted_iota(jnp.int32, (XROWS, 128), 0)
    ids_x = jnp.concatenate([ids_x, jnp.zeros((ids_x.shape[0], 128 - XROWS), F32)], axis=1)
    x_tile = jnp.where(row_x == 66, ids_x[2:3], jnp.where(row_x == 67, ids_x[3:4], x_tile))
    x_v[core, yh, z, :XROWS] = x_tile.astype(BF)
    x_own = x_v.at[core, yh, z, pl.ds(0, XROWS)]

    def x_copy(i):
        return rcopy(x_own, x_own, x_ss.at[i], x_rs.at[z], dp=(me_d + 4 * i) % DP)

    for i in (4, 3, 5, 2, 6, 1, 7):
        x_copy(i).start()

    def a_copy(o):
        return rcopy(send_v.at[o], recv_v.at[me_d], a_ss.at[o], a_rs.at[me_d], dp=o)

    def turn(i):
        return 4 + (2 * (i % 2) - 1) * ((i + 1) // 2)

    def a_step(i, carry):
        k = (z + turn(i)) % 8
        tile = dot(hot_v[k], items[...].reshape(B * F, 128))
        row = lax.broadcasted_iota(jnp.int32, (64, 128), 0)
        for q in range(4):
            o = k * 4 + q
            block = jnp.where(row == KEEP, meta_v[k, q:q + 1, :], tile[q * 64:(q + 1) * 64]).astype(BF)
            send_v[o] = block

            @pl.when(o == me_d)
            def _():
                recv_v[o] = block

            @pl.when(o != me_d)
            def _():
                a_copy(o).start()
        return carry

    rs_round(True, 1)
    rs_round(False, 3)
    lax.fori_loop(0, 4, a_step, 0)
    rs_round(True, 2)
    lax.fori_loop(4, 8, a_step, 0)
    rs_round(True, 3)

    tg_ref[...] = jnp.zeros_like(tg_ref)
    row_id = lax.broadcasted_iota(jnp.int32, (ROWS_DEV, 128), 0).astype(F32)

    def a_add(i, carry):
        k = (z + 8 - turn(i)) % 8
        low = lax.broadcasted_iota(jnp.int32, (8, 128), 1) < 64
        dead = lax.broadcasted_iota(jnp.int32, (8, 128), 1) % 64 >= KEEP
        for q in range(4):
            @pl.when(k * 4 + q != me_d)
            def _():
                rcopy(send_v.at[me_d], recv_v.at[k * 4 + q], a_ss.at[me_d], a_rs.at[k * 4 + q], dp=twin).wait_recv()
        ids = []
        for q in range(4):
            got = jnp.broadcast_to(recv_v[k * 4 + q, KEEP:KEEP + 1, :].astype(F32), (8, 128))
            swapped = pltpu.roll(got, 64, 1)
            ids.append(got + 256 * swapped if q % 2 == 0 else swapped + 256 * got)
        hots = []
        for m in range(2):
            both = jnp.where(dead, -1.0, jnp.where(low, ids[2 * m], ids[2 * m + 1]))[0:1]
            hots.append(jnp.where(row_id == both, 1.0, 0.0).astype(BF))
        values = recv_v[pl.ds(pl.multiple_of(k * 4, 4), 4)].reshape(256, 128)
        tg_ref[...] += dot(jnp.concatenate(hots, axis=1), values)
        return carry

    for i in range(1, 8):
        block = x_v.at[core, yh, (z + 8 - i) % 8, pl.ds(0, XROWS)]
        rcopy(block, block, x_ss.at[0], x_rs.at[(z + 8 - i) % 8], dp=twin).wait_recv()
    x_half = x_v.at[core, yh, :, pl.ds(0, XROWS)]
    start(rcopy(x_half, x_half, x_ss.at[8], x_rs.at[8], dp=y_part))

    lax.fori_loop(0, 4, a_add, 0)

    for way in range(2):
        for h in range(2):
            rs_copy(way, 3, h).wait_recv()

    def whole(h):
        return part(z, h) + rs_r[0, 3, h].astype(F32) + rs_r[1, 3, h].astype(F32)

    y_s[...] = whole(1 - yh).astype(BF)
    y_copy = rcopy(y_s, y_r, y_ss, y_rs, dp=y_part)
    start(y_copy)

    other = x_v.at[core, 1 - yh, :, pl.ds(0, XROWS)]
    rcopy(other, other, x_ss.at[8], x_rs.at[8], dp=y_part).wait_recv()
    x_all = x_v.at[core, :, :, pl.ds(0, XROWS)]
    start(rcopy(x_all, x_all, x_ss.at[9], x_rs.at[9], dp=twin))

    lax.fori_loop(4, 8, a_add, 0)
    last = whole(yh)
    y_copy.wait_recv()
    wg_ref[...] = (last + y_r[...].astype(F32)).astype(BF)

    x_twin = x_v.at[1 - core, :, :, pl.ds(0, XROWS)]
    rcopy(x_twin, x_twin, x_ss.at[9], x_rs.at[9], dp=twin).wait_recv()
    base = (me_d * ROWS_DEV).astype(F32)
    live = lax.broadcasted_iota(jnp.int32, (1, 128), 1) < 66

    def x_add(i, carry):
        hots = []
        for q in range(4):
            low = x_v[i // 4, (i // 2) % 2, (i % 2) * 4 + q, 66:67, :].astype(F32)
            high = x_v[i // 4, (i // 2) % 2, (i % 2) * 4 + q, 67:68, :].astype(F32)
            ids = jnp.where(live, low + 128 * high - base, -1.0)
            hots.append(jnp.where(row_id == ids, 1.0, 0.0).astype(BF))
        block = pl.ds(pl.multiple_of((i % 2) * 4, 4), 4)
        values = x_v[i // 4, (i // 2) % 2, block].reshape(512, 128)
        tg_ref[...] += dot(jnp.concatenate(hots, axis=1), values)
        return carry

    lax.fori_loop(0, 8, x_add, 0)

    for copy in sent:
        copy.wait_send()
    for i in range(1, 8):
        x_copy(i).wait_send()
    for way in range(2):
        for k in range(4):
            for h in range(2):
                if k > 0 or h == way:
                    rs_copy(way, k, h).wait_send()

    def drain(i, carry):
        a_copy((me_d + i) % DP).wait_send()
        return carry

    lax.fori_loop(1, DP, drain, 0)


def hand_over(wg_in, tg_in, wg_out, tg_out):
    wg_out[...] = wg_in[...]
    tg_out[...] = tg_in[...]


def on_device(embeddings, cotangent, first_weight, feature_rows):
    vmem = pl.BlockSpec(memory_space=pltpu.VMEM)
    hbm = pl.BlockSpec(memory_space=pl.ANY)
    dma = pltpu.SemaphoreType.DMA
    consts = [jnp.asarray(a) for a in constants()]
    shapes = (jax.ShapeDtypeStruct((2 * PAIRS, 256), BF), jax.ShapeDtypeStruct((ROWS_DEV, 128), F32))
    results = pl.pallas_call(
        kernel,
        out_shape=shapes,
        in_specs=[hbm, hbm, hbm, vmem, hbm, hbm, hbm],
        out_specs=(vmem, vmem),
        scratch_shapes=[
            pltpu.VMEM((2, B, 1024), BF),
            pltpu.VMEM((256, 256), BF),
            pltpu.VMEM((256, 128), BF),
            pltpu.VMEM((256, 256), BF),
            pltpu.VMEM((8, 2, 2, B, 256), BF),
            pltpu.VMEM((8, 2, B, 256), BF),
            pltpu.VMEM((2 * PAIRS, 8192), BF),
            pltpu.VMEM((F, B, 128), BF),
            pltpu.VMEM((F, B, 128), BF),
            pltpu.VMEM((B, 256), F32),
            pltpu.VMEM((2 * PAIRS, 256), BF),
            pltpu.VMEM((B, 256), F32),
            pltpu.VMEM((F, 128), jnp.int32),
            pltpu.VMEM((16, B * F), F32),
            pltpu.VMEM((8, 8, 128), F32),
            pltpu.VMEM((8, 256, B * F), BF),
            pltpu.VMEM((XROWS, B * F), BF),
            pltpu.VMEM((2, 4, 2, 2 * PAIRS, 256), BF),
            pltpu.VMEM((2, 4, 2, 2 * PAIRS, 256), BF),
            pltpu.VMEM((2 * PAIRS, 256), BF),
            pltpu.VMEM((2 * PAIRS, 256), BF),
            pltpu.VMEM((DP, 64, 128), BF),
            pltpu.VMEM((DP, 64, 128), BF),
            pltpu.VMEM((2, 2, 8, 128, 128), BF),
            dma((9,)), dma((11,)), dma((11,)), dma((8,)), dma((8,)), dma, dma,
            dma((2, 4, 2)), dma((2, 4, 2)), dma, dma,
            dma((DP,)), dma((DP,)), dma((10,)), dma((10,)),
        ],
        compiler_params=pltpu.CompilerParams(
            collective_id=0, has_side_effects=True, vmem_limit_bytes=56 * 1024 * 1024),
    )(embeddings, cotangent, first_weight, feature_rows.T, *consts)
    return pl.pallas_call(
        hand_over,
        out_shape=shapes,
        in_specs=[vmem, vmem],
        out_specs=(vmem, vmem),
    )(*results)


def solution(mesh):
    return jax.shard_map(
        on_device,
        mesh=mesh,
        in_specs=(P("set", "dp", None), P("dp", "set"), P("set", None), P("dp", None)),
        out_specs=(P("set", "dp"), P("dp", "set")),
        check_vma=False,
    )
```

```python
import functools

import jax
import jax.numpy as jnp
import numpy as np
from jax import lax
from jax.experimental import pallas as pl
from jax.experimental.pallas import tpu as pltpu
from jax.sharding import PartitionSpec as P

K = 64
F = 16
ROWS_DEV = 512
PAIRS = 120
B = 128
KEEP = 62
XROWS = 80
DP = 32
BF = jnp.bfloat16
F32 = jnp.float32
MESH = pl.DeviceIdType.MESH


def constants():
    first, second = np.triu_indices(F, 1)
    spread = np.zeros((256, F, 16), np.float32)
    mask = np.zeros((F, 16, 256), np.float32)
    for p in range(PAIRS):
        spread[p, second[p], :] = 1
        spread[128 + p, first[p], :] = 1
        mask[first[p], :, p] = 1
        mask[second[p], :, 128 + p] = 1
    spread = spread.reshape(256, 256)
    pick = np.ascontiguousarray(spread[:128].T)
    return [a.astype(BF) for a in (spread, pick, mask.reshape(256, 256))]


def dot(a, b):
    return jnp.dot(a, b, preferred_element_type=F32)


def dot_nt(a, b):
    return lax.dot_general(a, b, (((1,), (1,)), ((), ())), preferred_element_type=F32)


def kernel(emb_hbm, cot_ref, w_ref, rows_ref, spread_hbm, pick_hbm, mask_hbm, wg_ref, tg_ref,
           emb_ref, spread_ref, pick_ref, mask_ref,
           cot_v, cz_v, w_v, ei, items, pairs_v, pt_v, pg_v, pos_v, vals_v, meta_v,
           hot_v, hotx_v, wp_f, wp_s, wp_r, ws_s, ws_r, send_v, recv_v, x_v,
           loc_sem, ag_ss, ag_rs, cz_ss, cz_rs, pt_ss, pt_rs, wp_ss, wp_rs, ws_ss, ws_rs,
           a_ss, a_rs, x_ss, x_rs):
    me_s = lax.axis_index("set")
    me_d = lax.axis_index("dp")
    x, yl = me_s // 2, me_s % 2
    right = ((x + 1) % 4) * 2 + yl
    left = ((x + 3) % 4) * 2 + yl
    opp = ((x + 2) % 4) * 2 + yl
    over = me_s + 1 - 2 * yl
    right_o = right + 1 - 2 * yl
    left_o = left + 1 - 2 * yl
    opp_o = opp + 1 - 2 * yl
    z, yh, core = me_d // 4, (me_d // 2) % 2, me_d % 2
    twin = me_d + 1 - 2 * core
    y_part = me_d + 2 - 4 * yh
    unit = me_d % 4

    def rcopy(src, dst, ss, rs, **where):
        return pltpu.make_async_remote_copy(
            src_ref=src, dst_ref=dst, send_sem=ss, recv_sem=rs, device_id=where, device_id_type=MESH)

    own_copies = []
    for h in range(2):
        for cc in range(2):
            own_copies.append(pltpu.make_async_copy(
                cot_ref.at[:, pl.ds((h * 2 + cc) * 256, 256)], cot_v.at[me_s, cc, h], loc_sem.at[h * 2 + cc]))
    inputs = ((emb_hbm, emb_ref), (pick_hbm, pick_ref), (mask_hbm, mask_ref), (spread_hbm, spread_ref), (w_ref, w_v))
    in_copies = [pltpu.make_async_copy(a, b, loc_sem.at[4 + i]) for i, (a, b) in enumerate(inputs)]
    own_cz = pltpu.make_async_copy(cot_ref.at[:, pl.ds(pl.multiple_of(z * 128, 128), 128)],
                                   cz_v.at[me_s, z // 4, z % 4], loc_sem.at[9])
    for copy in own_copies + [own_cz] + in_copies:
        copy.start()

    barrier = pltpu.get_barrier_semaphore()
    for peer in (right, left, over):
        pl.semaphore_signal(barrier, inc=1, device_id={"set": peer}, device_id_type=MESH)

    def greet(i, carry):
        pl.semaphore_signal(barrier, inc=1, device_id={"dp": (me_d + i) % DP}, device_id_type=MESH)
        return carry

    lax.fori_loop(1, DP, greet, 0)
    for copy in own_copies:
        copy.wait()
    pl.semaphore_wait(barrier, 3 + DP - 1)

    sent = []

    def start(copy):
        copy.start()
        sent.append(copy)

    def ag(g, k, src, peer):
        start(rcopy(src, src, ag_ss.at[g, k], ag_rs.at[g, k], set=peer))

    def ag_wait(g, k, block):
        rcopy(block, block, ag_ss.at[g, k], ag_rs.at[g, k], set=right).wait_recv()

    def ag_own(g, buf):
        ag(g, 0, buf.at[me_s, 0], right)
        ag(g, 2, buf.at[me_s, 1], left)
        ag(g, 4, buf.at[me_s], over)
        ag(g, 1, buf.at[me_s, 1], right)
        ag(g, 3, buf.at[me_s, 0], left)

    def ag_halves(g, buf):
        ag_wait(g, 0, buf.at[left, 0])
        ag(g, 5, buf.at[left, 0], right)
        ag_wait(g, 2, buf.at[right, 1])
        ag(g, 6, buf.at[right, 1], left)

    def ag_over(g, buf):
        ag_wait(g, 4, buf.at[over])
        ag(g, 7, buf.at[over], right)
        ag(g, 8, buf.at[over], left)

    def ag_near(g, buf):
        ag_wait(g, 1, buf.at[left, 1])
        ag_wait(g, 3, buf.at[right, 0])

    def ag_opp(g, buf):
        ag_wait(g, 5, buf.at[opp, 0])
        ag(g, 9, buf.at[opp, 0], over)
        ag_wait(g, 6, buf.at[opp, 1])
        ag(g, 10, buf.at[opp, 1], over)

    def ag_opp_o(g, buf):
        ag_wait(g, 9, buf.at[opp_o, 0])
        ag_wait(g, 10, buf.at[opp_o, 1])

    ag_own(0, cot_v)

    def cz_copy(i):
        q = (z + i) % 8
        return rcopy(cot_ref.at[:, pl.ds(pl.multiple_of(q * 128, 128), 128)], cz_v.at[me_s, z // 4, z % 4],
                     cz_ss.at[i], cz_rs.at[z], dp=(me_d + 4 * i) % DP)

    far_first = (4, 3, 5, 2, 6, 1, 7)
    for i in far_first:
        start(cz_copy(i))

    for copy in in_copies[:4]:
        copy.wait()
    lane = lax.broadcasted_iota(jnp.int32, (B, 128), 1)
    for m in range(8):
        a = emb_ref[0, :, m * 128:(m + 1) * 128].astype(F32)
        b = emb_ref[1, :, m * 128:(m + 1) * 128].astype(F32)
        ei[2 * m] = jnp.where(lane < 64, a, pltpu.roll(b, 64, 1)).astype(BF)
        ei[2 * m + 1] = jnp.where(lane < 64, pltpu.roll(a, 64, 1), b).astype(BF)

    def diagonal():
        r = lax.broadcasted_iota(jnp.int32, (256, 256), 0)
        c = lax.broadcasted_iota(jnp.int32, (256, 256), 1)
        return (r % 16) == (c % 16)

    def group_rows(g):
        return pl.ds(pl.multiple_of(g * 16, 16), 16)

    def pair_step(g, carry):
        eg = ei[:, group_rows(g), :].reshape(256, 128)
        lane_g = lax.broadcasted_iota(jnp.int32, (256, 128), 1)
        for s in range(2):
            half = jnp.where((lane_g < 64) == (s == 0), eg.astype(F32), 0.0).astype(BF)
            gram = jnp.where(diagonal(), dot_nt(half, eg), 0.0).astype(BF)
            picked = dot(gram, pick_ref[...]) * mask_ref[:, :128].astype(F32)
            pairs_v[group_rows(g), s * 128:(s + 1) * 128] = jnp.sum(picked.reshape(F, 16, 128), axis=0)
        return carry

    lax.fori_loop(0, 4, pair_step, 0)

    ag_halves(0, cot_v)
    lax.fori_loop(4, 8, pair_step, 0)
    turned = pairs_v[...].T
    own_pairs = pl.ds(pl.multiple_of(z * B, B), B)
    pt_v[:, own_pairs] = jnp.concatenate([turned[:PAIRS], turned[128:128 + PAIRS]], axis=0).astype(BF)

    def pt_copy(i):
        return rcopy(pt_v.at[:, own_pairs], pt_v.at[:, own_pairs], pt_ss.at[i], pt_rs.at[z], dp=(me_d + 4 * i) % DP)

    for i in far_first:
        start(pt_copy(i))

    ag_over(0, cot_v)
    ag_near(0, cot_v)

    in_copies[4].wait()
    pg_v[...] = jnp.zeros_like(pg_v)

    def pg_add(j):
        total = None
        for h in range(2):
            for cc in range(2):
                cols = pl.ds(pl.multiple_of(j * 1024 + (h * 2 + cc) * 256, 256), 256)
                term = dot_nt(cot_v[j, cc, h], w_v[:, cols])
                total = term if total is None else total + term
        pg_v[:, :2 * PAIRS] += total

    def wp_copy(j, i):
        to = (unit + i) % 4
        return rcopy(wp_s.at[j, pl.ds(pl.multiple_of(to * 64, 64), 64)], wp_r.at[j, unit],
                     wp_ss.at[j, i], wp_rs.at[j, unit], dp=z * 4 + to)

    def wp_make(j):
        value = dot(pt_v[...], cz_v[j].reshape(8 * B, 128))
        value = jnp.concatenate([value, jnp.zeros((16, 128), F32)], axis=0)
        wp_f[j] = value
        wp_s[j] = value.astype(BF)
        for i in (2, 3, 1):
            start(wp_copy(j, i))

    def ws_copy(j):
        return rcopy(ws_s.at[j], ws_r.at[z % 2, unit], ws_ss.at[j], ws_rs.at[z % 2, unit], dp=j * 4 + z // 2)

    def ws_make(j):
        total = wp_f[j, pl.ds(pl.multiple_of(unit * 64, 64), 64)]
        for i in (1, 3, 2):
            source = (unit + i) % 4
            rcopy(wp_s.at[j, pl.ds(0, 64)], wp_r.at[j, source], wp_ss.at[j, i], wp_rs.at[j, source], dp=twin).wait_recv()
            total = total + wp_r[j, source].astype(F32)
        block = total.astype(BF)
        ws_s[j] = block
        here = j * 4 + z // 2 == me_d

        @pl.when(here)
        def _():
            ws_r[z % 2, unit] = block

        @pl.when(jnp.logical_not(here))
        def _():
            ws_copy(j).start()

    for j in (me_s, over, left, right):
        pg_add(j)

    ag_opp(0, cot_v)
    own_cz.wait()
    for i in range(1, 8):
        block = cz_v.at[me_s, ((z + i) % 8) // 4, (z + i) % 4]
        rcopy(block, block, cz_ss.at[i], cz_rs.at[(z + i) % 8], dp=twin).wait_recv()
    ag_own(1, cz_v)

    rows_t = rows_ref[...].astype(F32)
    owner = jnp.floor(rows_t * (1.0 / ROWS_DEV))
    local = rows_t - owner * ROWS_DEV
    local_hi = jnp.floor(local * (1.0 / 256))
    g_hi = jnp.floor(rows_t * (1.0 / 128))
    before = (lax.broadcasted_iota(jnp.int32, (128, 128), 0)
              < lax.broadcasted_iota(jnp.int32, (128, 128), 1)).astype(F32).astype(BF)
    owner_id = lax.broadcasted_iota(jnp.int32, (DP, 128), 0).astype(F32)
    seen = jnp.zeros((DP, 1), F32)
    vals_v[...] = jnp.zeros_like(vals_v)
    for f in range(F):
        hot = jnp.where(owner_id == owner[f:f + 1], 1.0, 0.0)
        earlier = dot(hot.astype(BF), before) + seen
        seen = seen + jnp.sum(hot, axis=1, keepdims=True)
        rank = jnp.sum(hot * earlier, axis=0, keepdims=True)
        pos = jnp.where(rank < KEEP, owner[f:f + 1] * 64 + rank, DP * 64 + rank - KEEP)
        pos_v[f:f + 1, :] = pos.astype(jnp.int32)
        cols = slice(f * 128, (f + 1) * 128)
        vals_v[0:1, cols] = local[f:f + 1] - 256 * local_hi[f:f + 1]
        vals_v[1:2, cols] = local_hi[f:f + 1]
        vals_v[2:3, cols] = rows_t[f:f + 1] - 128 * g_hi[f:f + 1]
        vals_v[3:4, cols] = g_hi[f:f + 1]

    def hot_step(k, carry):
        slot = lax.broadcasted_iota(jnp.int32, (256, 128), 0) + k * 256
        for f in range(F):
            hot_v[k, :, f * 128:(f + 1) * 128] = jnp.where(slot == pos_v[f:f + 1, :], 1.0, 0.0).astype(BF)
        ids = dot_nt(vals_v[...].astype(BF), hot_v[k])
        low = lax.broadcasted_iota(jnp.int32, (1, 128), 1) < 64
        for q in range(4):
            cols = slice((q // 2) * 128, (q // 2) * 128 + 128)
            lo, hi = ids[0:1, cols], ids[1:2, cols]
            if q % 2 == 0:
                row = jnp.where(low, lo, pltpu.roll(jnp.broadcast_to(hi, (8, 128)), 64, 1)[0:1])
            else:
                row = jnp.where(low, pltpu.roll(jnp.broadcast_to(lo, (8, 128)), 64, 1)[0:1], hi)
            meta_v[k, q:q + 1, :] = row
        return carry

    pg_add(opp)
    lax.fori_loop(0, 8, hot_step, 0)
    slot_x = lax.broadcasted_iota(jnp.int32, (XROWS, 128), 0) + DP * 64
    for f in range(F):
        hotx_v[:, f * 128:(f + 1) * 128] = jnp.where(slot_x == pos_v[f:f + 1, :], 1.0, 0.0).astype(BF)
    ids_x = dot_nt(vals_v[...].astype(BF), hotx_v[...])
    x_v[:, :, :, XROWS:] = jnp.zeros((2, 2, 8, 128 - XROWS, 128), BF)

    ag_opp_o(0, cot_v)
    pg_add(opp_o)
    ag_wait(0, 7, cot_v.at[left_o])
    ag_wait(0, 8, cot_v.at[right_o])
    pg_add(left_o)
    pg_add(right_o)

    pg_all = pg_v[...]
    pg_v[...] = pg_all.astype(BF).astype(F32)

    def emb_step(g, carry):
        eg = ei[:, group_rows(g), :].reshape(256, 128)
        a = pg_v[group_rows(g), :]
        grads = []
        for s in range(2):
            one = (a if s == 0 else pltpu.roll(a, 256 - PAIRS, 1))[:, :128]
            both = jnp.concatenate([one, one], axis=1).astype(BF)
            tall = jnp.concatenate([both] * F, axis=0) * mask_ref[...]
            sym = jnp.where(diagonal(), dot(tall, spread_ref[...]), 0.0).astype(BF)
            grads.append(dot(sym, eg))
        lane_g = lax.broadcasted_iota(jnp.int32, (256, 128), 1)
        items[:, group_rows(g), :] = jnp.where(lane_g < 64, grads[0], grads[1]).astype(BF).reshape(F, 16, 128)
        return carry

    lax.fori_loop(0, 2, emb_step, 0, unroll=2)
    ag_halves(1, cz_v)
    lax.fori_loop(2, 8, emb_step, 0, unroll=3)
    ag_over(1, cz_v)

    x_tile = dot(hotx_v[...], items[...].reshape(B * F, 128))
    row_x = lax.broadcasted_iota(jnp.int32, (XROWS, 128), 0)
    ids_x = jnp.concatenate([ids_x, jnp.zeros((ids_x.shape[0], 128 - XROWS), F32)], axis=1)
    x_tile = jnp.where(row_x == 66, ids_x[2:3], jnp.where(row_x == 67, ids_x[3:4], x_tile))
    x_v[core, yh, z, :XROWS] = x_tile.astype(BF)
    x_own = x_v.at[core, yh, z, pl.ds(0, XROWS)]

    def x_copy(i):
        return rcopy(x_own, x_own, x_ss.at[i], x_rs.at[z], dp=(me_d + 4 * i) % DP)

    for i in far_first:
        start(x_copy(i))

    def a_copy(o):
        return rcopy(send_v.at[o], recv_v.at[me_d], a_ss.at[o], a_rs.at[me_d], dp=o)

    def turn(i):
        return 4 + (2 * (i % 2) - 1) * ((i + 1) // 2)

    def a_step(i, carry):
        k = (z + turn(i)) % 8
        tile = dot(hot_v[k], items[...].reshape(B * F, 128))
        row = lax.broadcasted_iota(jnp.int32, (64, 128), 0)
        for q in range(4):
            o = k * 4 + q
            block = jnp.where(row == KEEP, meta_v[k, q:q + 1, :], tile[q * 64:(q + 1) * 64]).astype(BF)
            send_v[o] = block

            @pl.when(o == me_d)
            def _():
                recv_v[o] = block

            @pl.when(o != me_d)
            def _():
                a_copy(o).start()
        return carry

    lax.fori_loop(0, 4, a_step, 0)
    ag_near(1, cz_v)
    ag_opp(1, cz_v)
    lax.fori_loop(4, 8, a_step, 0)

    for i in range(1, 8):
        block = pt_v.at[:, pl.ds(pl.multiple_of((z + i) % 8 * B, B), B)]
        rcopy(block, block, pt_ss.at[i], pt_rs.at[(z + i) % 8], dp=twin).wait_recv()
    early = (me_s, over, left, right, opp)
    for j in early:
        wp_make(j)

    tg_ref[...] = jnp.zeros_like(tg_ref)
    row_id = lax.broadcasted_iota(jnp.int32, (ROWS_DEV, 128), 0).astype(F32)

    def a_add(i, carry):
        k = (z + 8 - turn(i)) % 8
        low = lax.broadcasted_iota(jnp.int32, (8, 128), 1) < 64
        dead = lax.broadcasted_iota(jnp.int32, (8, 128), 1) % 64 >= KEEP
        for q in range(4):
            @pl.when(k * 4 + q != me_d)
            def _():
                rcopy(send_v.at[me_d], recv_v.at[k * 4 + q], a_ss.at[me_d], a_rs.at[k * 4 + q], dp=twin).wait_recv()
        ids = []
        for q in range(4):
            got = jnp.broadcast_to(recv_v[k * 4 + q, KEEP:KEEP + 1, :].astype(F32), (8, 128))
            swapped = pltpu.roll(got, 64, 1)
            ids.append(got + 256 * swapped if q % 2 == 0 else swapped + 256 * got)
        hots = []
        for m in range(2):
            both = jnp.where(dead, -1.0, jnp.where(low, ids[2 * m], ids[2 * m + 1]))[0:1]
            hots.append(jnp.where(row_id == both, 1.0, 0.0).astype(BF))
        values = recv_v[pl.ds(pl.multiple_of(k * 4, 4), 4)].reshape(256, 128)
        tg_ref[...] += dot(jnp.concatenate(hots, axis=1), values)
        return carry

    for i in range(1, 8):
        block = x_v.at[core, yh, (z + 8 - i) % 8, pl.ds(0, XROWS)]
        rcopy(block, block, x_ss.at[0], x_rs.at[(z + 8 - i) % 8], dp=twin).wait_recv()
    x_half = x_v.at[core, yh, :, pl.ds(0, XROWS)]
    start(rcopy(x_half, x_half, x_ss.at[8], x_rs.at[8], dp=y_part))

    ag_opp_o(1, cz_v)
    wp_make(opp_o)
    ag_wait(1, 7, cz_v.at[left_o])
    wp_make(left_o)
    ag_wait(1, 8, cz_v.at[right_o])
    wp_make(right_o)
    for j in early:
        ws_make(j)
    lax.fori_loop(0, 4, a_add, 0)
    for j in (opp_o, left_o, right_o):
        ws_make(j)

    other = x_v.at[core, 1 - yh, :, pl.ds(0, XROWS)]
    rcopy(other, other, x_ss.at[8], x_rs.at[8], dp=y_part).wait_recv()
    x_all = x_v.at[core, :, :, pl.ds(0, XROWS)]
    start(rcopy(x_all, x_all, x_ss.at[9], x_rs.at[9], dp=twin))

    lax.fori_loop(4, 8, a_add, 0)

    base = (me_d * ROWS_DEV).astype(F32)
    live = lax.broadcasted_iota(jnp.int32, (1, 128), 1) < 66

    def x_add(cc):
        def body(i, carry):
            half, first = i // 2, (i % 2) * 4
            hots = []
            for q in range(4):
                low = x_v[cc, half, first + q, 66:67, :].astype(F32)
                high = x_v[cc, half, first + q, 67:68, :].astype(F32)
                ids = jnp.where(live, low + 128 * high - base, -1.0)
                hots.append(jnp.where(row_id == ids, 1.0, 0.0).astype(BF))
            values = x_v[cc, half, pl.ds(pl.multiple_of(first, 4), 4)].reshape(512, 128)
            tg_ref[...] += dot(jnp.concatenate(hots, axis=1), values)
            return carry

        lax.fori_loop(0, 4, body, 0)

    x_add(core)
    x_twin = x_v.at[1 - core, :, :, pl.ds(0, XROWS)]
    rcopy(x_twin, x_twin, x_ss.at[9], x_rs.at[9], dp=twin).wait_recv()
    x_add(1 - core)

    for half in range(2):
        for source in range(4):
            @pl.when((unit * 2 + half) * 4 + source != me_d)
            def _():
                rcopy(ws_s.at[0], ws_r.at[half, source], ws_ss.at[0], ws_rs.at[half, source], dp=twin).wait_recv()

            rows = min(64, 2 * PAIRS - source * 64)
            wg_ref[source * 64:source * 64 + rows, half * 128:(half + 1) * 128] = ws_r[half, source, :rows]

    for copy in sent:
        copy.wait_send()
    for j in range(8):
        @pl.when(j * 4 + z // 2 != me_d)
        def _():
            ws_copy(j).wait_send()

    def drain(i, carry):
        a_copy((me_d + i) % DP).wait_send()
        return carry

    lax.fori_loop(1, DP, drain, 0)


def hand_over(wg_in, tg_in, wg_out, tg_out):
    wg_out[...] = wg_in[...]
    tg_out[...] = tg_in[...]


def on_device(embeddings, cotangent, first_weight, feature_rows):
    vmem = pl.BlockSpec(memory_space=pltpu.VMEM)
    hbm = pl.BlockSpec(memory_space=pl.ANY)
    dma = pltpu.SemaphoreType.DMA
    consts = [jnp.asarray(a) for a in constants()]
    shapes = (jax.ShapeDtypeStruct((2 * PAIRS, 256), BF), jax.ShapeDtypeStruct((ROWS_DEV, 128), F32))
    results = pl.pallas_call(
        kernel,
        out_shape=shapes,
        in_specs=[hbm, hbm, hbm, vmem, hbm, hbm, hbm],
        out_specs=(vmem, vmem),
        scratch_shapes=[
            pltpu.VMEM((2, B, 1024), BF),
            pltpu.VMEM((256, 256), BF),
            pltpu.VMEM((256, 128), BF),
            pltpu.VMEM((256, 256), BF),
            pltpu.VMEM((8, 2, 2, B, 256), BF),
            pltpu.VMEM((8, 2, 4, B, 128), BF),
            pltpu.VMEM((2 * PAIRS, 8192), BF),
            pltpu.VMEM((F, B, 128), BF),
            pltpu.VMEM((F, B, 128), BF),
            pltpu.VMEM((B, 256), F32),
            pltpu.VMEM((2 * PAIRS, 8 * B), BF),
            pltpu.VMEM((B, 256), F32),
            pltpu.VMEM((F, 128), jnp.int32),
            pltpu.VMEM((16, B * F), F32),
            pltpu.VMEM((8, 8, 128), F32),
            pltpu.VMEM((8, 256, B * F), BF),
            pltpu.VMEM((XROWS, B * F), BF),
            pltpu.VMEM((8, 256, 128), F32),
            pltpu.VMEM((8, 256, 128), BF),
            pltpu.VMEM((8, 4, 64, 128), BF),
            pltpu.VMEM((8, 64, 128), BF),
            pltpu.VMEM((2, 4, 64, 128), BF),
            pltpu.VMEM((DP, 64, 128), BF),
            pltpu.VMEM((DP, 64, 128), BF),
            pltpu.VMEM((2, 2, 8, 128, 128), BF),
            dma((10,)), dma((2, 11)), dma((2, 11)), dma((8,)), dma((8,)), dma((8,)), dma((8,)),
            dma((8, 4)), dma((8, 4)), dma((8,)), dma((2, 4)),
            dma((DP,)), dma((DP,)), dma((10,)), dma((10,)),
        ],
        compiler_params=pltpu.CompilerParams(
            collective_id=0, has_side_effects=True, vmem_limit_bytes=56 * 1024 * 1024),
    )(embeddings, cotangent, first_weight, feature_rows.T, *consts)
    return pl.pallas_call(
        hand_over,
        out_shape=shapes,
        in_specs=[vmem, vmem],
        out_specs=(vmem, vmem),
    )(*results)


def solution(mesh):
    return jax.shard_map(
        on_device,
        mesh=mesh,
        in_specs=(P("set", "dp", None), P("dp", "set"), P("set", None), P("dp", None)),
        out_specs=(P("set", "dp"), P("dp", "set")),
        check_vma=False,
    )
```

```python
import functools

import jax
import jax.numpy as jnp
import numpy as np
from jax import lax
from jax.experimental import pallas as pl
from jax.experimental.pallas import tpu as pltpu
from jax.sharding import PartitionSpec as P

K = 64
F = 16
ROWS_DEV = 512
PAIRS = 120
B = 128
KEEP = 62
XROWS = 80
DP = 32
BF = jnp.bfloat16
F32 = jnp.float32
MESH = pl.DeviceIdType.MESH


def constants():
    first, second = np.triu_indices(F, 1)
    spread = np.zeros((256, F, 16), np.float32)
    mask = np.zeros((F, 16, 256), np.float32)
    for p in range(PAIRS):
        spread[p, second[p], :] = 1
        spread[128 + p, first[p], :] = 1
        mask[first[p], :, p] = 1
        mask[second[p], :, 128 + p] = 1
    spread = spread.reshape(256, 256)
    pick = np.ascontiguousarray(spread[:128].T)
    return [a.astype(BF) for a in (spread, pick, mask.reshape(256, 256))]


def dot(a, b):
    return jnp.dot(a, b, preferred_element_type=F32)


def dot_nt(a, b):
    return lax.dot_general(a, b, (((1,), (1,)), ((), ())), preferred_element_type=F32)


def kernel(emb_hbm, cot_ref, w_ref, rows_ref, spread_hbm, pick_hbm, mask_hbm, wg_ref, tg_ref,
           emb_ref, spread_ref, pick_ref, mask_ref,
           cot_v, cz_v, w_v, ei, items, pairs_v, pt_v, pg_v, pos_v, vals_v, meta_v,
           hot_v, hotx_v, wp_f, wp_s, wp_r, ws_s, ws_r, wl_s, wl_r, send_v, recv_v, x_v,
           loc_sem, ag_ss, ag_rs, cz_ss, cz_rs, pt_ss, pt_rs, wp_ss, wp_rs, ws_ss, ws_rs, wl_ss, wl_rs,
           a_ss, a_rs, x_ss, x_rs):
    me_s = lax.axis_index("set")
    me_d = lax.axis_index("dp")
    x, yl = me_s // 2, me_s % 2
    right = ((x + 1) % 4) * 2 + yl
    left = ((x + 3) % 4) * 2 + yl
    opp = ((x + 2) % 4) * 2 + yl
    over = me_s + 1 - 2 * yl
    right_o = right + 1 - 2 * yl
    left_o = left + 1 - 2 * yl
    opp_o = opp + 1 - 2 * yl
    z, yh, core = me_d // 4, (me_d // 2) % 2, me_d % 2
    twin = me_d + 1 - 2 * core
    y_part = me_d + 2 - 4 * yh
    unit = me_d % 4

    def rcopy(src, dst, ss, rs, **where):
        return pltpu.make_async_remote_copy(
            src_ref=src, dst_ref=dst, send_sem=ss, recv_sem=rs, device_id=where, device_id_type=MESH)

    own_copies = []
    for h in range(2):
        for cc in range(2):
            own_copies.append(pltpu.make_async_copy(
                cot_ref.at[:, pl.ds((h * 2 + cc) * 256, 256)], cot_v.at[me_s, cc, h], loc_sem.at[h * 2 + cc]))
    inputs = ((emb_hbm, emb_ref), (pick_hbm, pick_ref), (mask_hbm, mask_ref), (spread_hbm, spread_ref), (w_ref, w_v))
    in_copies = [pltpu.make_async_copy(a, b, loc_sem.at[4 + i]) for i, (a, b) in enumerate(inputs)]
    own_cz = pltpu.make_async_copy(cot_ref.at[:, pl.ds(pl.multiple_of(z * 128, 128), 128)],
                                   cz_v.at[me_s, z // 4, z % 4], loc_sem.at[9])
    for copy in own_copies + [own_cz] + in_copies:
        copy.start()

    barrier = pltpu.get_barrier_semaphore()
    for peer in (right, left, over):
        pl.semaphore_signal(barrier, inc=1, device_id={"set": peer}, device_id_type=MESH)

    def greet(i, carry):
        pl.semaphore_signal(barrier, inc=1, device_id={"dp": (me_d + i) % DP}, device_id_type=MESH)
        return carry

    lax.fori_loop(1, DP, greet, 0)
    for copy in own_copies:
        copy.wait()
    pl.semaphore_wait(barrier, 3 + DP - 1)

    sent = []

    def start(copy):
        copy.start()
        sent.append(copy)

    def ag(g, k, src, peer):
        start(rcopy(src, src, ag_ss.at[g, k], ag_rs.at[g, k], set=peer))

    def ag_wait(g, k, block):
        rcopy(block, block, ag_ss.at[g, k], ag_rs.at[g, k], set=right).wait_recv()

    def ag_own(g, buf):
        ag(g, 0, buf.at[me_s, 0], right)
        ag(g, 2, buf.at[me_s, 1], left)
        ag(g, 4, buf.at[me_s], over)
        ag(g, 1, buf.at[me_s, 1], right)
        ag(g, 3, buf.at[me_s, 0], left)

    def ag_halves(g, buf):
        ag_wait(g, 0, buf.at[left, 0])
        ag(g, 5, buf.at[left, 0], right)
        ag_wait(g, 2, buf.at[right, 1])
        ag(g, 6, buf.at[right, 1], left)

    def ag_over(g, buf):
        ag_wait(g, 4, buf.at[over])
        ag(g, 7, buf.at[over], right)
        ag(g, 8, buf.at[over], left)

    def ag_near(g, buf):
        ag_wait(g, 1, buf.at[left, 1])
        ag_wait(g, 3, buf.at[right, 0])

    def ag_opp(g, buf):
        ag_wait(g, 5, buf.at[opp, 0])
        ag(g, 9, buf.at[opp, 0], over)
        ag_wait(g, 6, buf.at[opp, 1])
        ag(g, 10, buf.at[opp, 1], over)

    def ag_opp_o(g, buf):
        ag_wait(g, 9, buf.at[opp_o, 0])
        ag_wait(g, 10, buf.at[opp_o, 1])

    ag_own(0, cot_v)

    def cz_copy(i):
        q = (z + i) % 8
        return rcopy(cot_ref.at[:, pl.ds(pl.multiple_of(q * 128, 128), 128)], cz_v.at[me_s, z // 4, z % 4],
                     cz_ss.at[i], cz_rs.at[z], dp=(me_d + 4 * i) % DP)

    far_first = (4, 3, 5, 2, 6, 1, 7)
    for i in far_first:
        start(cz_copy(i))

    for copy in in_copies[:4]:
        copy.wait()
    lane = lax.broadcasted_iota(jnp.int32, (B, 128), 1)
    for m in range(8):
        a = emb_ref[0, :, m * 128:(m + 1) * 128].astype(F32)
        b = emb_ref[1, :, m * 128:(m + 1) * 128].astype(F32)
        ei[2 * m] = jnp.where(lane < 64, a, pltpu.roll(b, 64, 1)).astype(BF)
        ei[2 * m + 1] = jnp.where(lane < 64, pltpu.roll(a, 64, 1), b).astype(BF)

    def diagonal():
        r = lax.broadcasted_iota(jnp.int32, (256, 256), 0)
        c = lax.broadcasted_iota(jnp.int32, (256, 256), 1)
        return (r % 16) == (c % 16)

    def group_rows(g):
        return pl.ds(pl.multiple_of(g * 16, 16), 16)

    def pair_step(g, carry):
        eg = ei[:, group_rows(g), :].reshape(256, 128)
        lane_g = lax.broadcasted_iota(jnp.int32, (256, 128), 1)
        for s in range(2):
            half = jnp.where((lane_g < 64) == (s == 0), eg.astype(F32), 0.0).astype(BF)
            gram = jnp.where(diagonal(), dot_nt(half, eg), 0.0).astype(BF)
            picked = dot(gram, pick_ref[...]) * mask_ref[:, :128].astype(F32)
            pairs_v[group_rows(g), s * 128:(s + 1) * 128] = jnp.sum(picked.reshape(F, 16, 128), axis=0)
        return carry

    lax.fori_loop(0, 4, pair_step, 0)

    ag_halves(0, cot_v)
    lax.fori_loop(4, 8, pair_step, 0)
    turned = pairs_v[...].T
    own_pairs = pl.ds(pl.multiple_of(z * B, B), B)
    pt_v[:, own_pairs] = jnp.concatenate([turned[:PAIRS], turned[128:128 + PAIRS]], axis=0).astype(BF)

    def pt_copy(i):
        return rcopy(pt_v.at[:, own_pairs], pt_v.at[:, own_pairs], pt_ss.at[i], pt_rs.at[z], dp=(me_d + 4 * i) % DP)

    for i in far_first:
        start(pt_copy(i))

    ag_over(0, cot_v)
    ag_near(0, cot_v)

    in_copies[4].wait()
    pg_v[...] = jnp.zeros_like(pg_v)

    def pg_add(j):
        total = None
        for h in range(2):
            for cc in range(2):
                cols = pl.ds(pl.multiple_of(j * 1024 + (h * 2 + cc) * 256, 256), 256)
                term = dot_nt(cot_v[j, cc, h], w_v[:, cols])
                total = term if total is None else total + term
        pg_v[:, :2 * PAIRS] += total

    def wp_copy(j, i):
        to = (unit + i) % 4
        return rcopy(wp_s.at[j, pl.ds(pl.multiple_of(to * 64, 64), 64)], wp_r.at[j, unit],
                     wp_ss.at[j, i], wp_rs.at[j, unit], dp=z * 4 + to)

    def wp_make(j):
        value = dot(pt_v[...], cz_v[j].reshape(8 * B, 128))
        value = jnp.concatenate([value, jnp.zeros((16, 128), F32)], axis=0)
        wp_f[j] = value
        wp_s[j] = value.astype(BF)
        for i in (2, 3, 1):
            start(wp_copy(j, i))

    def ws_copy(j):
        return rcopy(ws_s.at[j], ws_r.at[z % 2, unit], ws_ss.at[j], ws_rs.at[z % 2, unit], dp=j * 4 + z // 2)

    def ws_make(j):
        total = wp_f[j, pl.ds(pl.multiple_of(unit * 64, 64), 64)]
        for i in (1, 3, 2):
            source = (unit + i) % 4
            rcopy(wp_s.at[j, pl.ds(0, 64)], wp_r.at[j, source], wp_ss.at[j, i], wp_rs.at[j, source], dp=twin).wait_recv()
            total = total + wp_r[j, source].astype(F32)
        block = total.astype(BF)
        ws_s[j] = block
        here = j * 4 + z // 2 == me_d

        @pl.when(here)
        def _():
            ws_r[z % 2, unit] = block

        @pl.when(jnp.logical_not(here))
        def _():
            ws_copy(j).start()

    late = (opp_o, left_o, right_o)
    late_here = (z == opp_o) | (z == left_o) | (z == right_o)

    def wl_copy(t):
        return rcopy(wl_s.at[t], wl_r.at[z % 2, unit], wl_ss.at[t], wl_rs.at[z % 2, unit], dp=late[t] * 4 + z // 2)

    def wl_make(t):
        block = dot(pt_v[...], cz_v[late[t]].reshape(8 * B, 128)).astype(BF)
        wl_s[t] = block
        here = late[t] * 4 + z // 2 == me_d

        @pl.when(here)
        def _():
            wl_r[z % 2, unit] = block

        @pl.when(jnp.logical_not(here))
        def _():
            wl_copy(t).start()

    for j in (me_s, over, left, right):
        pg_add(j)

    ag_opp(0, cot_v)
    own_cz.wait()
    for i in range(1, 8):
        block = cz_v.at[me_s, ((z + i) % 8) // 4, (z + i) % 4]
        rcopy(block, block, cz_ss.at[i], cz_rs.at[(z + i) % 8], dp=twin).wait_recv()
    ag_own(1, cz_v)

    rows_t = rows_ref[...].astype(F32)
    owner = jnp.floor(rows_t * (1.0 / ROWS_DEV))
    local = rows_t - owner * ROWS_DEV
    local_hi = jnp.floor(local * (1.0 / 256))
    g_hi = jnp.floor(rows_t * (1.0 / 128))
    before = (lax.broadcasted_iota(jnp.int32, (128, 128), 0)
              < lax.broadcasted_iota(jnp.int32, (128, 128), 1)).astype(F32).astype(BF)
    owner_id = lax.broadcasted_iota(jnp.int32, (DP, 128), 0).astype(F32)
    seen = jnp.zeros((DP, 1), F32)
    vals_v[...] = jnp.zeros_like(vals_v)
    for f in range(F):
        hot = jnp.where(owner_id == owner[f:f + 1], 1.0, 0.0)
        earlier = dot(hot.astype(BF), before) + seen
        seen = seen + jnp.sum(hot, axis=1, keepdims=True)
        rank = jnp.sum(hot * earlier, axis=0, keepdims=True)
        pos = jnp.where(rank < KEEP, owner[f:f + 1] * 64 + rank, DP * 64 + rank - KEEP)
        pos_v[f:f + 1, :] = pos.astype(jnp.int32)
        cols = slice(f * 128, (f + 1) * 128)
        vals_v[0:1, cols] = local[f:f + 1] - 256 * local_hi[f:f + 1]
        vals_v[1:2, cols] = local_hi[f:f + 1]
        vals_v[2:3, cols] = rows_t[f:f + 1] - 128 * g_hi[f:f + 1]
        vals_v[3:4, cols] = g_hi[f:f + 1]

    def hot_step(k, carry):
        slot = lax.broadcasted_iota(jnp.int32, (256, 128), 0) + k * 256
        for f in range(F):
            hot_v[k, :, f * 128:(f + 1) * 128] = jnp.where(slot == pos_v[f:f + 1, :], 1.0, 0.0).astype(BF)
        ids = dot_nt(vals_v[...].astype(BF), hot_v[k])
        low = lax.broadcasted_iota(jnp.int32, (1, 128), 1) < 64
        for q in range(4):
            cols = slice((q // 2) * 128, (q // 2) * 128 + 128)
            lo, hi = ids[0:1, cols], ids[1:2, cols]
            if q % 2 == 0:
                row = jnp.where(low, lo, pltpu.roll(jnp.broadcast_to(hi, (8, 128)), 64, 1)[0:1])
            else:
                row = jnp.where(low, pltpu.roll(jnp.broadcast_to(lo, (8, 128)), 64, 1)[0:1], hi)
            meta_v[k, q:q + 1, :] = row
        return carry

    pg_add(opp)
    lax.fori_loop(0, 8, hot_step, 0)
    slot_x = lax.broadcasted_iota(jnp.int32, (XROWS, 128), 0) + DP * 64
    for f in range(F):
        hotx_v[:, f * 128:(f + 1) * 128] = jnp.where(slot_x == pos_v[f:f + 1, :], 1.0, 0.0).astype(BF)
    ids_x = dot_nt(vals_v[...].astype(BF), hotx_v[...])
    x_v[:, :, :, XROWS:] = jnp.zeros((2, 2, 8, 128 - XROWS, 128), BF)

    ag_opp_o(0, cot_v)
    pg_add(opp_o)
    ag_wait(0, 7, cot_v.at[left_o])
    ag_wait(0, 8, cot_v.at[right_o])
    pg_add(left_o)
    pg_add(right_o)

    pg_all = pg_v[...]
    pg_v[...] = pg_all.astype(BF).astype(F32)

    def emb_step(g, carry):
        eg = ei[:, group_rows(g), :].reshape(256, 128)
        a = pg_v[group_rows(g), :]
        grads = []
        for s in range(2):
            one = (a if s == 0 else pltpu.roll(a, 256 - PAIRS, 1))[:, :128]
            both = jnp.concatenate([one, one], axis=1).astype(BF)
            tall = jnp.concatenate([both] * F, axis=0) * mask_ref[...]
            sym = jnp.where(diagonal(), dot(tall, spread_ref[...]), 0.0).astype(BF)
            grads.append(dot(sym, eg))
        lane_g = lax.broadcasted_iota(jnp.int32, (256, 128), 1)
        items[:, group_rows(g), :] = jnp.where(lane_g < 64, grads[0], grads[1]).astype(BF).reshape(F, 16, 128)
        return carry

    lax.fori_loop(0, 2, emb_step, 0, unroll=2)
    ag_halves(1, cz_v)
    lax.fori_loop(2, 8, emb_step, 0, unroll=3)
    ag_over(1, cz_v)
    for i in range(1, 8):
        block = pt_v.at[:, pl.ds(pl.multiple_of((z + i) % 8 * B, B), B)]
        rcopy(block, block, pt_ss.at[i], pt_rs.at[(z + i) % 8], dp=twin).wait_recv()
    wp_make(me_s)

    x_tile = dot(hotx_v[...], items[...].reshape(B * F, 128))
    row_x = lax.broadcasted_iota(jnp.int32, (XROWS, 128), 0)
    ids_x = jnp.concatenate([ids_x, jnp.zeros((ids_x.shape[0], 128 - XROWS), F32)], axis=1)
    x_tile = jnp.where(row_x == 66, ids_x[2:3], jnp.where(row_x == 67, ids_x[3:4], x_tile))
    x_v[core, yh, z, :XROWS] = x_tile.astype(BF)
    x_own = x_v.at[core, yh, z, pl.ds(0, XROWS)]

    def x_copy(i):
        return rcopy(x_own, x_own, x_ss.at[i], x_rs.at[z], dp=(me_d + 4 * i) % DP)

    for i in far_first:
        start(x_copy(i))

    def a_copy(o):
        return rcopy(send_v.at[o], recv_v.at[me_d], a_ss.at[o], a_rs.at[me_d], dp=o)

    def turn(i):
        return 4 + (2 * (i % 2) - 1) * ((i + 1) // 2)

    def a_step(i, carry):
        k = (z + turn(i)) % 8
        tile = dot(hot_v[k], items[...].reshape(B * F, 128))
        row = lax.broadcasted_iota(jnp.int32, (64, 128), 0)
        for q in range(4):
            o = k * 4 + q
            block = jnp.where(row == KEEP, meta_v[k, q:q + 1, :], tile[q * 64:(q + 1) * 64]).astype(BF)
            send_v[o] = block

            @pl.when(o == me_d)
            def _():
                recv_v[o] = block

            @pl.when(o != me_d)
            def _():
                a_copy(o).start()
        return carry

    lax.fori_loop(0, 2, a_step, 0)
    ag_near(1, cz_v)
    for j in (over, left, right):
        wp_make(j)
    lax.fori_loop(2, 5, a_step, 0)
    ag_opp(1, cz_v)
    wp_make(opp)
    lax.fori_loop(5, 8, a_step, 0)

    ws_make(me_s)
    for j in (over, left, right):
        ws_make(j)

    tg_ref[...] = jnp.zeros_like(tg_ref)
    row_id = lax.broadcasted_iota(jnp.int32, (ROWS_DEV, 128), 0).astype(F32)

    def a_add(i, carry):
        k = (z + 8 - turn(i)) % 8
        low = lax.broadcasted_iota(jnp.int32, (8, 128), 1) < 64
        dead = lax.broadcasted_iota(jnp.int32, (8, 128), 1) % 64 >= KEEP
        for q in range(4):
            @pl.when(k * 4 + q != me_d)
            def _():
                rcopy(send_v.at[me_d], recv_v.at[k * 4 + q], a_ss.at[me_d], a_rs.at[k * 4 + q], dp=twin).wait_recv()
        ids = []
        for q in range(4):
            got = jnp.broadcast_to(recv_v[k * 4 + q, KEEP:KEEP + 1, :].astype(F32), (8, 128))
            swapped = pltpu.roll(got, 64, 1)
            ids.append(got + 256 * swapped if q % 2 == 0 else swapped + 256 * got)
        hots = []
        for m in range(2):
            both = jnp.where(dead, -1.0, jnp.where(low, ids[2 * m], ids[2 * m + 1]))[0:1]
            hots.append(jnp.where(row_id == both, 1.0, 0.0).astype(BF))
        values = recv_v[pl.ds(pl.multiple_of(k * 4, 4), 4)].reshape(256, 128)
        tg_ref[...] += dot(jnp.concatenate(hots, axis=1), values)
        return carry

    ag_opp_o(1, cz_v)
    wl_make(0)
    ag_wait(1, 7, cz_v.at[left_o])
    wl_make(1)
    ag_wait(1, 8, cz_v.at[right_o])
    wl_make(2)
    for i in range(1, 8):
        block = x_v.at[core, yh, (z + 8 - i) % 8, pl.ds(0, XROWS)]
        rcopy(block, block, x_ss.at[0], x_rs.at[(z + 8 - i) % 8], dp=twin).wait_recv()
    x_half = x_v.at[core, yh, :, pl.ds(0, XROWS)]
    start(rcopy(x_half, x_half, x_ss.at[8], x_rs.at[8], dp=y_part))

    ws_make(opp)
    lax.fori_loop(0, 4, a_add, 0)

    other = x_v.at[core, 1 - yh, :, pl.ds(0, XROWS)]
    rcopy(other, other, x_ss.at[8], x_rs.at[8], dp=y_part).wait_recv()
    x_all = x_v.at[core, :, :, pl.ds(0, XROWS)]
    start(rcopy(x_all, x_all, x_ss.at[9], x_rs.at[9], dp=twin))

    lax.fori_loop(4, 8, a_add, 0)

    base = (me_d * ROWS_DEV).astype(F32)
    live = lax.broadcasted_iota(jnp.int32, (1, 128), 1) < 66

    def x_add(cc):
        def body(i, carry):
            half, first = i // 2, (i % 2) * 4
            hots = []
            for q in range(4):
                low = x_v[cc, half, first + q, 66:67, :].astype(F32)
                high = x_v[cc, half, first + q, 67:68, :].astype(F32)
                ids = jnp.where(live, low + 128 * high - base, -1.0)
                hots.append(jnp.where(row_id == ids, 1.0, 0.0).astype(BF))
            values = x_v[cc, half, pl.ds(pl.multiple_of(first, 4), 4)].reshape(512, 128)
            tg_ref[...] += dot(jnp.concatenate(hots, axis=1), values)
            return carry

        lax.fori_loop(0, 4, body, 0)

    x_add(core)
    x_twin = x_v.at[1 - core, :, :, pl.ds(0, XROWS)]
    rcopy(x_twin, x_twin, x_ss.at[9], x_rs.at[9], dp=twin).wait_recv()
    x_add(1 - core)

    def from_line(half, source, block, arrived):
        @pl.when((unit * 2 + half) * 4 + source != me_d)
        def _():
            rcopy(block, block, ws_ss.at[0], arrived, dp=twin).wait_recv()

    @pl.when(late_here)
    def _():
        for half in range(2):
            total = None
            for source in range(4):
                from_line(half, source, wl_r.at[half, source], wl_rs.at[half, source])
                term = wl_r[half, source].astype(F32)
                total = term if total is None else total + term
            wg_ref[:, half * 128:(half + 1) * 128] = total.astype(BF)

    @pl.when(jnp.logical_not(late_here))
    def _():
        for half in range(2):
            for source in range(4):
                from_line(half, source, ws_r.at[half, source], ws_rs.at[half, source])
                rows = min(64, 2 * PAIRS - source * 64)
                wg_ref[source * 64:source * 64 + rows, half * 128:(half + 1) * 128] = ws_r[half, source, :rows]

    for copy in sent:
        copy.wait_send()
    for j in (me_s, over, left, right, opp):
        @pl.when(j * 4 + z // 2 != me_d)
        def _():
            ws_copy(j).wait_send()
    for t in range(3):
        @pl.when(late[t] * 4 + z // 2 != me_d)
        def _():
            wl_copy(t).wait_send()

    def drain(i, carry):
        a_copy((me_d + i) % DP).wait_send()
        return carry

    lax.fori_loop(1, DP, drain, 0)


def hand_over(wg_in, tg_in, wg_out, tg_out):
    wg_out[...] = wg_in[...]
    tg_out[...] = tg_in[...]


def on_device(embeddings, cotangent, first_weight, feature_rows):
    vmem = pl.BlockSpec(memory_space=pltpu.VMEM)
    hbm = pl.BlockSpec(memory_space=pl.ANY)
    dma = pltpu.SemaphoreType.DMA
    consts = [jnp.asarray(a) for a in constants()]
    shapes = (jax.ShapeDtypeStruct((2 * PAIRS, 256), BF), jax.ShapeDtypeStruct((ROWS_DEV, 128), F32))
    results = pl.pallas_call(
        kernel,
        out_shape=(pltpu.VMEM((2 * PAIRS, 256), BF), pltpu.VMEM((ROWS_DEV, 128), F32)),
        in_specs=[hbm, hbm, hbm, vmem, hbm, hbm, hbm],
        out_specs=(vmem, vmem),
        scratch_shapes=[
            pltpu.VMEM((2, B, 1024), BF),
            pltpu.VMEM((256, 256), BF),
            pltpu.VMEM((256, 128), BF),
            pltpu.VMEM((256, 256), BF),
            pltpu.VMEM((8, 2, 2, B, 256), BF),
            pltpu.VMEM((8, 2, 4, B, 128), BF),
            pltpu.VMEM((2 * PAIRS, 8192), BF),
            pltpu.VMEM((F, B, 128), BF),
            pltpu.VMEM((F, B, 128), BF),
            pltpu.VMEM((B, 256), F32),
            pltpu.VMEM((2 * PAIRS, 8 * B), BF),
            pltpu.VMEM((B, 256), F32),
            pltpu.VMEM((F, 128), jnp.int32),
            pltpu.VMEM((16, B * F), F32),
            pltpu.VMEM((8, 8, 128), F32),
            pltpu.VMEM((8, 256, B * F), BF),
            pltpu.VMEM((XROWS, B * F), BF),
            pltpu.VMEM((8, 256, 128), F32),
            pltpu.VMEM((8, 256, 128), BF),
            pltpu.VMEM((8, 4, 64, 128), BF),
            pltpu.VMEM((8, 64, 128), BF),
            pltpu.VMEM((2, 4, 64, 128), BF),
            pltpu.VMEM((3, 2 * PAIRS, 128), BF),
            pltpu.VMEM((2, 4, 2 * PAIRS, 128), BF),
            pltpu.VMEM((DP, 64, 128), BF),
            pltpu.VMEM((DP, 64, 128), BF),
            pltpu.VMEM((2, 2, 8, 128, 128), BF),
            dma((10,)), dma((2, 11)), dma((2, 11)), dma((8,)), dma((8,)), dma((8,)), dma((8,)),
            dma((8, 4)), dma((8, 4)), dma((8,)), dma((2, 4)), dma((3,)), dma((2, 4)),
            dma((DP,)), dma((DP,)), dma((10,)), dma((10,)),
        ],
        compiler_params=pltpu.CompilerParams(
            collective_id=0, has_side_effects=True, vmem_limit_bytes=56 * 1024 * 1024),
    )(embeddings, cotangent, first_weight, feature_rows.T, *consts)
    return pl.pallas_call(
        hand_over,
        out_shape=shapes,
        in_specs=[vmem, vmem],
        out_specs=(vmem, vmem),
    )(*[pltpu.with_memory_space_constraint(r, pltpu.VMEM) for r in results])


def solution(mesh):
    return jax.shard_map(
        on_device,
        mesh=mesh,
        in_specs=(P("set", "dp", None), P("dp", "set"), P("set", None), P("dp", None)),
        out_specs=(P("set", "dp"), P("dp", "set")),
        check_vma=False,
    )
```

```python
import functools

import jax
import jax.numpy as jnp
import numpy as np
from jax import lax
from jax.experimental import pallas as pl
from jax.experimental.pallas import tpu as pltpu
from jax.sharding import PartitionSpec as P

K = 64
F = 16
ROWS_DEV = 512
PAIRS = 120
B = 128
KEEP = 62
XROWS = 80
DP = 32
BF = jnp.bfloat16
F32 = jnp.float32
MESH = pl.DeviceIdType.MESH


def constants():
    first, second = np.triu_indices(F, 1)
    spread = np.zeros((256, F, 16), np.float32)
    mask = np.zeros((F, 16, 256), np.float32)
    for p in range(PAIRS):
        spread[p, second[p], :] = 1
        spread[128 + p, first[p], :] = 1
        mask[first[p], :, p] = 1
        mask[second[p], :, 128 + p] = 1
    spread = spread.reshape(256, 256)
    pick = np.ascontiguousarray(spread[:128].T)
    return [a.astype(BF) for a in (spread, pick, mask.reshape(256, 256))]


def dot(a, b):
    return jnp.dot(a, b, preferred_element_type=F32)


def dot_nt(a, b):
    return lax.dot_general(a, b, (((1,), (1,)), ((), ())), preferred_element_type=F32)


def kernel(emb_hbm, cot_ref, w_ref, rows_ref, spread_hbm, pick_hbm, mask_hbm, wg_ref, tg_ref,
           emb_ref, spread_ref, pick_ref, mask_ref,
           cot_v, cz_v, w_v, ei, items, pairs_v, pt_v, pg_v, pos_v, vals_v, meta_v,
           hot_v, hotx_v, wp_f, wp_s, wp_r, ws_s, ws_r, wl_s, wl_r, send_v, recv_v, x_v,
           loc_sem, ag_ss, ag_rs, cz_ss, cz_rs, pt_ss, pt_rs, wp_ss, wp_rs, ws_ss, ws_rs, wl_ss, wl_rs,
           a_ss, a_rs, x_ss, x_rs):
    me_s = lax.axis_index("set")
    me_d = lax.axis_index("dp")
    x, yl = me_s // 2, me_s % 2
    right = ((x + 1) % 4) * 2 + yl
    left = ((x + 3) % 4) * 2 + yl
    opp = ((x + 2) % 4) * 2 + yl
    over = me_s + 1 - 2 * yl
    right_o = right + 1 - 2 * yl
    left_o = left + 1 - 2 * yl
    opp_o = opp + 1 - 2 * yl
    z, yh, core = me_d // 4, (me_d // 2) % 2, me_d % 2
    twin = me_d + 1 - 2 * core
    y_part = me_d + 2 - 4 * yh
    unit = me_d % 4

    def rcopy(src, dst, ss, rs, **where):
        return pltpu.make_async_remote_copy(
            src_ref=src, dst_ref=dst, send_sem=ss, recv_sem=rs, device_id=where, device_id_type=MESH)

    own_copies = []
    for h in range(2):
        for cc in range(2):
            own_copies.append(pltpu.make_async_copy(
                cot_ref.at[:, pl.ds((h * 2 + cc) * 256, 256)], cot_v.at[me_s, cc, h], loc_sem.at[h * 2 + cc]))
    inputs = ((emb_hbm, emb_ref), (pick_hbm, pick_ref), (mask_hbm, mask_ref), (spread_hbm, spread_ref), (w_ref, w_v))
    in_copies = [pltpu.make_async_copy(a, b, loc_sem.at[4 + i]) for i, (a, b) in enumerate(inputs)]
    own_cz = pltpu.make_async_copy(cot_ref.at[:, pl.ds(pl.multiple_of(z * 128, 128), 128)],
                                   cz_v.at[me_s, z // 4, z % 4], loc_sem.at[9])
    for copy in own_copies + [own_cz] + in_copies:
        copy.start()

    barrier = pltpu.get_barrier_semaphore()
    for peer in (right, left, over):
        pl.semaphore_signal(barrier, inc=1, device_id={"set": peer}, device_id_type=MESH)

    def greet(i, carry):
        pl.semaphore_signal(barrier, inc=1, device_id={"dp": (me_d + i) % DP}, device_id_type=MESH)
        return carry

    lax.fori_loop(1, DP, greet, 0)
    for copy in own_copies:
        copy.wait()
    pl.semaphore_wait(barrier, 3 + DP - 1)

    sent = []

    def start(copy):
        copy.start()
        sent.append(copy)

    def settle():
        for copy in sent:
            copy.wait_send()
        sent.clear()

    def ag(g, k, src, peer):
        start(rcopy(src, src, ag_ss.at[g, k], ag_rs.at[g, k], set=peer))

    def ag_wait(g, k, block):
        rcopy(block, block, ag_ss.at[g, k], ag_rs.at[g, k], set=right).wait_recv()

    def ag_own(g, buf):
        ag(g, 0, buf.at[me_s, 0], right)
        ag(g, 2, buf.at[me_s, 1], left)
        ag(g, 4, buf.at[me_s], over)
        ag(g, 1, buf.at[me_s, 1], right)
        ag(g, 3, buf.at[me_s, 0], left)

    def ag_halves(g, buf):
        ag_wait(g, 0, buf.at[left, 0])
        ag(g, 5, buf.at[left, 0], right)
        ag_wait(g, 2, buf.at[right, 1])
        ag(g, 6, buf.at[right, 1], left)

    def ag_over(g, buf):
        ag_wait(g, 4, buf.at[over])
        ag(g, 7, buf.at[over], right)
        ag(g, 8, buf.at[over], left)

    def ag_near(g, buf):
        ag_wait(g, 1, buf.at[left, 1])
        ag_wait(g, 3, buf.at[right, 0])

    def ag_opp(g, buf):
        ag_wait(g, 5, buf.at[opp, 0])
        if g == 0:
            ag(g, 9, buf.at[opp, 0], over)
        ag_wait(g, 6, buf.at[opp, 1])
        if g == 0:
            ag(g, 10, buf.at[opp, 1], over)

    def ag_opp_o(g, buf):
        ag_wait(g, 9, buf.at[opp_o, 0])
        ag_wait(g, 10, buf.at[opp_o, 1])

    ag_own(0, cot_v)

    def cz_copy(i):
        q = (z + i) % 8
        return rcopy(cot_ref.at[:, pl.ds(pl.multiple_of(q * 128, 128), 128)], cz_v.at[me_s, z // 4, z % 4],
                     cz_ss.at[i], cz_rs.at[z], dp=(me_d + 4 * i) % DP)

    far_first = (4, 3, 5, 2, 6, 1, 7)
    for i in far_first:
        start(cz_copy(i))

    for copy in in_copies[:4]:
        copy.wait()
    lane = lax.broadcasted_iota(jnp.int32, (B, 128), 1)
    for m in range(8):
        a = emb_ref[0, :, m * 128:(m + 1) * 128].astype(F32)
        b = emb_ref[1, :, m * 128:(m + 1) * 128].astype(F32)
        ei[2 * m] = jnp.where(lane < 64, a, pltpu.roll(b, 64, 1)).astype(BF)
        ei[2 * m + 1] = jnp.where(lane < 64, pltpu.roll(a, 64, 1), b).astype(BF)

    def diagonal():
        r = lax.broadcasted_iota(jnp.int32, (256, 256), 0)
        c = lax.broadcasted_iota(jnp.int32, (256, 256), 1)
        return (r % 16) == (c % 16)

    def group_rows(g):
        return pl.ds(pl.multiple_of(g * 16, 16), 16)

    def pair_step(g, carry):
        eg = ei[:, group_rows(g), :].reshape(256, 128)
        lane_g = lax.broadcasted_iota(jnp.int32, (256, 128), 1)
        for s in range(2):
            half = jnp.where((lane_g < 64) == (s == 0), eg.astype(F32), 0.0).astype(BF)
            gram = jnp.where(diagonal(), dot_nt(half, eg), 0.0).astype(BF)
            picked = dot(gram, pick_ref[...]) * mask_ref[:, :128].astype(F32)
            pairs_v[group_rows(g), s * 128:(s + 1) * 128] = jnp.sum(picked.reshape(F, 16, 128), axis=0)
        return carry

    lax.fori_loop(0, 4, pair_step, 0)

    ag_halves(0, cot_v)
    lax.fori_loop(4, 8, pair_step, 0)
    turned = pairs_v[...].T
    own_pairs = pl.ds(pl.multiple_of(z * B, B), B)
    pt_v[:, own_pairs] = jnp.concatenate([turned[:PAIRS], turned[128:128 + PAIRS]], axis=0).astype(BF)

    def pt_copy(i):
        return rcopy(pt_v.at[:, own_pairs], pt_v.at[:, own_pairs], pt_ss.at[i], pt_rs.at[z], dp=(me_d + 4 * i) % DP)

    for i in far_first:
        start(pt_copy(i))

    ag_over(0, cot_v)
    ag_near(0, cot_v)

    in_copies[4].wait()
    pg_v[...] = jnp.zeros_like(pg_v)

    def pg_add(j):
        total = None
        for h in range(2):
            for cc in range(2):
                cols = pl.ds(pl.multiple_of(j * 1024 + (h * 2 + cc) * 256, 256), 256)
                term = dot_nt(cot_v[j, cc, h], w_v[:, cols])
                total = term if total is None else total + term
        pg_v[:, :2 * PAIRS] += total

    def wp_copy(j, i):
        to = (unit + i) % 4
        return rcopy(wp_s.at[j, pl.ds(pl.multiple_of(to * 64, 64), 64)], wp_r.at[j, unit],
                     wp_ss.at[j, i], wp_rs.at[j, unit], dp=z * 4 + to)

    def wp_make(j):
        value = dot(pt_v[...], cz_v[j].reshape(8 * B, 128))
        value = jnp.concatenate([value, jnp.zeros((16, 128), F32)], axis=0)
        wp_f[j] = value
        wp_s[j] = value.astype(BF)
        for i in (2, 3, 1):
            start(wp_copy(j, i))

    def ws_copy(j):
        return rcopy(ws_s.at[j], ws_r.at[z % 2, unit], ws_ss.at[j], ws_rs.at[z % 2, unit], dp=j * 4 + z // 2)

    def ws_make(j):
        total = wp_f[j, pl.ds(pl.multiple_of(unit * 64, 64), 64)]
        for i in (1, 3, 2):
            source = (unit + i) % 4
            rcopy(wp_s.at[j, pl.ds(0, 64)], wp_r.at[j, source], wp_ss.at[j, i], wp_rs.at[j, source], dp=twin).wait_recv()
            total = total + wp_r[j, source].astype(F32)
        block = total.astype(BF)
        ws_s[j] = block
        here = j * 4 + z // 2 == me_d

        @pl.when(here)
        def _():
            ws_r[z % 2, unit] = block

        @pl.when(jnp.logical_not(here))
        def _():
            ws_copy(j).start()

    late = (opp_o, left_o, right_o)
    late_here = (z == opp_o) | (z == left_o) | (z == right_o)

    def wl_copy(t):
        return rcopy(wl_s.at[t], wl_r.at[z % 2, unit], wl_ss.at[t], wl_rs.at[z % 2, unit], dp=late[t] * 4 + z // 2)

    def wl_make(t):
        block = dot(pt_v[...], cz_v[late[t]].reshape(8 * B, 128)).astype(BF)
        wl_s[t] = block
        here = late[t] * 4 + z // 2 == me_d

        @pl.when(here)
        def _():
            wl_r[z % 2, unit] = block

        @pl.when(jnp.logical_not(here))
        def _():
            wl_copy(t).start()

    for j in (me_s, over, left, right):
        pg_add(j)

    ag_opp(0, cot_v)
    own_cz.wait()
    for i in range(1, 8):
        block = cz_v.at[me_s, ((z + i) % 8) // 4, (z + i) % 4]
        rcopy(block, block, cz_ss.at[i], cz_rs.at[(z + i) % 8], dp=twin).wait_recv()
    ag_own(1, cz_v)

    rows_t = rows_ref[...].astype(F32)
    owner = jnp.floor(rows_t * (1.0 / ROWS_DEV))
    local = rows_t - owner * ROWS_DEV
    local_hi = jnp.floor(local * (1.0 / 256))
    g_hi = jnp.floor(rows_t * (1.0 / 128))
    before = (lax.broadcasted_iota(jnp.int32, (128, 128), 0)
              < lax.broadcasted_iota(jnp.int32, (128, 128), 1)).astype(F32).astype(BF)
    owner_id = lax.broadcasted_iota(jnp.int32, (DP, 128), 0).astype(F32)
    seen = jnp.zeros((DP, 1), F32)
    vals_v[...] = jnp.zeros_like(vals_v)
    for f in range(F):
        hot = jnp.where(owner_id == owner[f:f + 1], 1.0, 0.0)
        earlier = dot(hot.astype(BF), before) + seen
        seen = seen + jnp.sum(hot, axis=1, keepdims=True)
        rank = jnp.sum(hot * earlier, axis=0, keepdims=True)
        pos = jnp.where(rank < KEEP, owner[f:f + 1] * 64 + rank, DP * 64 + rank - KEEP)
        pos_v[f:f + 1, :] = pos.astype(jnp.int32)
        cols = slice(f * 128, (f + 1) * 128)
        vals_v[0:1, cols] = local[f:f + 1] - 256 * local_hi[f:f + 1]
        vals_v[1:2, cols] = local_hi[f:f + 1]
        vals_v[2:3, cols] = rows_t[f:f + 1] - 128 * g_hi[f:f + 1]
        vals_v[3:4, cols] = g_hi[f:f + 1]

    def hot_step(k, carry):
        slot = lax.broadcasted_iota(jnp.int32, (256, 128), 0) + k * 256
        for f in range(F):
            hot_v[k, :, f * 128:(f + 1) * 128] = jnp.where(slot == pos_v[f:f + 1, :], 1.0, 0.0).astype(BF)
        ids = dot_nt(vals_v[...].astype(BF), hot_v[k])
        low = lax.broadcasted_iota(jnp.int32, (1, 128), 1) < 64
        for q in range(4):
            cols = slice((q // 2) * 128, (q // 2) * 128 + 128)
            lo, hi = ids[0:1, cols], ids[1:2, cols]
            if q % 2 == 0:
                row = jnp.where(low, lo, pltpu.roll(jnp.broadcast_to(hi, (8, 128)), 64, 1)[0:1])
            else:
                row = jnp.where(low, pltpu.roll(jnp.broadcast_to(lo, (8, 128)), 64, 1)[0:1], hi)
            meta_v[k, q:q + 1, :] = row
        return carry

    pg_add(opp)
    lax.fori_loop(0, 8, hot_step, 0)
    slot_x = lax.broadcasted_iota(jnp.int32, (XROWS, 128), 0) + DP * 64
    for f in range(F):
        hotx_v[:, f * 128:(f + 1) * 128] = jnp.where(slot_x == pos_v[f:f + 1, :], 1.0, 0.0).astype(BF)
    ids_x = dot_nt(vals_v[...].astype(BF), hotx_v[...])
    x_v[:, :, :, XROWS:] = jnp.zeros((2, 2, 8, 128 - XROWS, 128), BF)

    ag_opp_o(0, cot_v)
    pg_add(opp_o)
    ag_wait(0, 7, cot_v.at[left_o])
    ag_wait(0, 8, cot_v.at[right_o])
    pg_add(left_o)
    pg_add(right_o)

    pg_all = pg_v[...]
    pg_v[...] = pg_all.astype(BF).astype(F32)

    def emb_step(g, carry):
        eg = ei[:, group_rows(g), :].reshape(256, 128)
        a = pg_v[group_rows(g), :]
        grads = []
        for s in range(2):
            one = (a if s == 0 else pltpu.roll(a, 256 - PAIRS, 1))[:, :128]
            both = jnp.concatenate([one, one], axis=1).astype(BF)
            tall = jnp.concatenate([both] * F, axis=0) * mask_ref[...]
            sym = jnp.where(diagonal(), dot(tall, spread_ref[...]), 0.0).astype(BF)
            grads.append(dot(sym, eg))
        lane_g = lax.broadcasted_iota(jnp.int32, (256, 128), 1)
        items[:, group_rows(g), :] = jnp.where(lane_g < 64, grads[0], grads[1]).astype(BF).reshape(F, 16, 128)
        return carry

    lax.fori_loop(0, 2, emb_step, 0, unroll=2)
    ag_halves(1, cz_v)
    lax.fori_loop(2, 8, emb_step, 0, unroll=3)
    ag_over(1, cz_v)
    for i in range(1, 8):
        block = pt_v.at[:, pl.ds(pl.multiple_of((z + i) % 8 * B, B), B)]
        rcopy(block, block, pt_ss.at[i], pt_rs.at[(z + i) % 8], dp=twin).wait_recv()
    wp_make(me_s)

    x_tile = dot(hotx_v[...], items[...].reshape(B * F, 128))
    row_x = lax.broadcasted_iota(jnp.int32, (XROWS, 128), 0)
    ids_x = jnp.concatenate([ids_x, jnp.zeros((ids_x.shape[0], 128 - XROWS), F32)], axis=1)
    x_tile = jnp.where(row_x == 66, ids_x[2:3], jnp.where(row_x == 67, ids_x[3:4], x_tile))
    x_v[core, yh, z, :XROWS] = x_tile.astype(BF)
    x_own = x_v.at[core, yh, z, pl.ds(0, XROWS)]

    def x_copy(i):
        return rcopy(x_own, x_own, x_ss.at[i], x_rs.at[z], dp=(me_d + 4 * i) % DP)

    for i in far_first:
        start(x_copy(i))

    def a_copy(o):
        return rcopy(send_v.at[o], recv_v.at[me_d], a_ss.at[o], a_rs.at[me_d], dp=o)

    def turn(i):
        return 4 + (2 * (i % 2) - 1) * ((i + 1) // 2)

    def a_step(i, carry):
        k = (z + turn(i)) % 8
        tile = dot(hot_v[k], items[...].reshape(B * F, 128))
        row = lax.broadcasted_iota(jnp.int32, (64, 128), 0)
        for q in range(4):
            o = k * 4 + q
            block = jnp.where(row == KEEP, meta_v[k, q:q + 1, :], tile[q * 64:(q + 1) * 64]).astype(BF)
            send_v[o] = block

            @pl.when(o == me_d)
            def _():
                recv_v[o] = block

            @pl.when(o != me_d)
            def _():
                a_copy(o).start()
        return carry

    lax.fori_loop(0, 2, a_step, 0)
    ag_near(1, cz_v)
    for j in (over, left, right):
        wp_make(j)
    lax.fori_loop(2, 5, a_step, 0)
    ag_opp(1, cz_v)
    wp_make(opp)
    lax.fori_loop(5, 8, a_step, 0)

    ws_make(me_s)
    for j in (over, left, right):
        ws_make(j)

    tg_ref[...] = jnp.zeros_like(tg_ref)
    row_id = lax.broadcasted_iota(jnp.int32, (ROWS_DEV, 128), 0).astype(F32)

    def a_add(i, carry):
        k = (z + 8 - turn(i)) % 8
        low = lax.broadcasted_iota(jnp.int32, (8, 128), 1) < 64
        dead = lax.broadcasted_iota(jnp.int32, (8, 128), 1) % 64 >= KEEP
        for q in range(4):
            @pl.when(k * 4 + q != me_d)
            def _():
                rcopy(send_v.at[me_d], recv_v.at[k * 4 + q], a_ss.at[me_d], a_rs.at[k * 4 + q], dp=twin).wait_recv()
        ids = []
        for q in range(4):
            got = jnp.broadcast_to(recv_v[k * 4 + q, KEEP:KEEP + 1, :].astype(F32), (8, 128))
            swapped = pltpu.roll(got, 64, 1)
            ids.append(got + 256 * swapped if q % 2 == 0 else swapped + 256 * got)
        hots = []
        for m in range(2):
            both = jnp.where(dead, -1.0, jnp.where(low, ids[2 * m], ids[2 * m + 1]))[0:1]
            hots.append(jnp.where(row_id == both, 1.0, 0.0).astype(BF))
        values = recv_v[pl.ds(pl.multiple_of(k * 4, 4), 4)].reshape(256, 128)
        tg_ref[...] += dot(jnp.concatenate(hots, axis=1), values)
        return carry

    ag_wait(1, 7, cz_v.at[left_o])
    ag(1, 9, cz_v.at[left_o, 0], right)
    ag_wait(1, 8, cz_v.at[right_o])
    ag(1, 10, cz_v.at[right_o, 1], left)
    wl_make(1)
    wl_make(2)
    ag_opp_o(1, cz_v)
    wl_make(0)
    settle()
    for i in range(1, 8):
        block = x_v.at[core, yh, (z + 8 - i) % 8, pl.ds(0, XROWS)]
        rcopy(block, block, x_ss.at[0], x_rs.at[(z + 8 - i) % 8], dp=twin).wait_recv()
    x_half = x_v.at[core, yh, :, pl.ds(0, XROWS)]
    start(rcopy(x_half, x_half, x_ss.at[8], x_rs.at[8], dp=y_part))

    ws_make(opp)
    lax.fori_loop(0, 4, a_add, 0)

    other = x_v.at[core, 1 - yh, :, pl.ds(0, XROWS)]
    rcopy(other, other, x_ss.at[8], x_rs.at[8], dp=y_part).wait_recv()
    x_all = x_v.at[core, :, :, pl.ds(0, XROWS)]
    start(rcopy(x_all, x_all, x_ss.at[9], x_rs.at[9], dp=twin))

    lax.fori_loop(4, 8, a_add, 0)

    base = (me_d * ROWS_DEV).astype(F32)
    live = lax.broadcasted_iota(jnp.int32, (1, 128), 1) < 66

    def x_add(cc):
        def body(i, carry):
            half, first = i // 2, (i % 2) * 4
            hots = []
            for q in range(4):
                low = x_v[cc, half, first + q, 66:67, :].astype(F32)
                high = x_v[cc, half, first + q, 67:68, :].astype(F32)
                ids = jnp.where(live, low + 128 * high - base, -1.0)
                hots.append(jnp.where(row_id == ids, 1.0, 0.0).astype(BF))
            values = x_v[cc, half, pl.ds(pl.multiple_of(first, 4), 4)].reshape(512, 128)
            tg_ref[...] += dot(jnp.concatenate(hots, axis=1), values)
            return carry

        lax.fori_loop(0, 4, body, 0)

    x_add(core)
    x_twin = x_v.at[1 - core, :, :, pl.ds(0, XROWS)]
    rcopy(x_twin, x_twin, x_ss.at[9], x_rs.at[9], dp=twin).wait_recv()
    x_add(1 - core)

    def drain(i, carry):
        a_copy((me_d + i) % DP).wait_send()
        return carry

    lax.fori_loop(1, DP, drain, 0)

    def from_line(half, source, block, arrived):
        @pl.when((unit * 2 + half) * 4 + source != me_d)
        def _():
            rcopy(block, block, ws_ss.at[0], arrived, dp=twin).wait_recv()

    @pl.when(late_here)
    def _():
        for half in range(2):
            total = None
            for source in range(4):
                from_line(half, source, wl_r.at[half, source], wl_rs.at[half, source])
                term = wl_r[half, source].astype(F32)
                total = term if total is None else total + term
            wg_ref[:, half * 128:(half + 1) * 128] = total.astype(BF)

    @pl.when(jnp.logical_not(late_here))
    def _():
        for half in range(2):
            for source in range(4):
                from_line(half, source, ws_r.at[half, source], ws_rs.at[half, source])
                rows = min(64, 2 * PAIRS - source * 64)
                wg_ref[source * 64:source * 64 + rows, half * 128:(half + 1) * 128] = ws_r[half, source, :rows]

    settle()
    for j in (me_s, over, left, right, opp):
        @pl.when(j * 4 + z // 2 != me_d)
        def _():
            ws_copy(j).wait_send()
    for t in range(3):
        @pl.when(late[t] * 4 + z // 2 != me_d)
        def _():
            wl_copy(t).wait_send()


def hand_over(wg_in, tg_in, wg_out, tg_out):
    wg_out[...] = wg_in[...]
    tg_out[...] = tg_in[...]


def on_device(embeddings, cotangent, first_weight, feature_rows):
    vmem = pl.BlockSpec(memory_space=pltpu.VMEM)
    hbm = pl.BlockSpec(memory_space=pl.ANY)
    dma = pltpu.SemaphoreType.DMA
    consts = [jnp.asarray(a) for a in constants()]
    shapes = (jax.ShapeDtypeStruct((2 * PAIRS, 256), BF), jax.ShapeDtypeStruct((ROWS_DEV, 128), F32))
    results = pl.pallas_call(
        kernel,
        out_shape=(pltpu.VMEM((2 * PAIRS, 256), BF), pltpu.VMEM((ROWS_DEV, 128), F32)),
        in_specs=[hbm, hbm, hbm, vmem, hbm, hbm, hbm],
        out_specs=(vmem, vmem),
        scratch_shapes=[
            pltpu.VMEM((2, B, 1024), BF),
            pltpu.VMEM((256, 256), BF),
            pltpu.VMEM((256, 128), BF),
            pltpu.VMEM((256, 256), BF),
            pltpu.VMEM((8, 2, 2, B, 256), BF),
            pltpu.VMEM((8, 2, 4, B, 128), BF),
            pltpu.VMEM((2 * PAIRS, 8192), BF),
            pltpu.VMEM((F, B, 128), BF),
            pltpu.VMEM((F, B, 128), BF),
            pltpu.VMEM((B, 256), F32),
            pltpu.VMEM((2 * PAIRS, 8 * B), BF),
            pltpu.VMEM((B, 256), F32),
            pltpu.VMEM((F, 128), jnp.int32),
            pltpu.VMEM((16, B * F), F32),
            pltpu.VMEM((8, 8, 128), F32),
            pltpu.VMEM((8, 256, B * F), BF),
            pltpu.VMEM((XROWS, B * F), BF),
            pltpu.VMEM((8, 256, 128), F32),
            pltpu.VMEM((8, 256, 128), BF),
            pltpu.VMEM((8, 4, 64, 128), BF),
            pltpu.VMEM((8, 64, 128), BF),
            pltpu.VMEM((2, 4, 64, 128), BF),
            pltpu.VMEM((3, 2 * PAIRS, 128), BF),
            pltpu.VMEM((2, 4, 2 * PAIRS, 128), BF),
            pltpu.VMEM((DP, 64, 128), BF),
            pltpu.VMEM((DP, 64, 128), BF),
            pltpu.VMEM((2, 2, 8, 128, 128), BF),
            dma((10,)), dma((2, 11)), dma((2, 11)), dma((8,)), dma((8,)), dma((8,)), dma((8,)),
            dma((8, 4)), dma((8, 4)), dma((8,)), dma((2, 4)), dma((3,)), dma((2, 4)),
            dma((DP,)), dma((DP,)), dma((10,)), dma((10,)),
        ],
        compiler_params=pltpu.CompilerParams(
            collective_id=0, has_side_effects=True, vmem_limit_bytes=56 * 1024 * 1024),
    )(embeddings, cotangent, first_weight, feature_rows.T, *consts)
    return pl.pallas_call(
        hand_over,
        out_shape=shapes,
        in_specs=[vmem, vmem],
        out_specs=(vmem, vmem),
    )(*[pltpu.with_memory_space_constraint(r, pltpu.VMEM) for r in results])


def solution(mesh):
    return jax.shard_map(
        on_device,
        mesh=mesh,
        in_specs=(P("set", "dp", None), P("dp", "set"), P("set", None), P("dp", None)),
        out_specs=(P("set", "dp"), P("dp", "set")),
        check_vma=False,
    )
```

```python
import functools

import jax
import jax.numpy as jnp
import numpy as np
from jax import lax
from jax.experimental import pallas as pl
from jax.experimental.pallas import tpu as pltpu
from jax.sharding import PartitionSpec as P

K = 64
F = 16
ROWS_DEV = 512
PAIRS = 120
B = 128
KEEP = 62
XROWS = 80
DP = 32
BF = jnp.bfloat16
F32 = jnp.float32
MESH = pl.DeviceIdType.MESH


def constants():
    first, second = np.triu_indices(F, 1)
    spread = np.zeros((256, F, 16), np.float32)
    mask = np.zeros((F, 16, 256), np.float32)
    for p in range(PAIRS):
        spread[p, second[p], :] = 1
        spread[128 + p, first[p], :] = 1
        mask[first[p], :, p] = 1
        mask[second[p], :, 128 + p] = 1
    spread = spread.reshape(256, 256)
    pick = np.ascontiguousarray(spread[:128].T)
    return [a.astype(BF) for a in (spread, pick, mask.reshape(256, 256))]


def dot(a, b):
    return jnp.dot(a, b, preferred_element_type=F32)


def dot_nt(a, b):
    return lax.dot_general(a, b, (((1,), (1,)), ((), ())), preferred_element_type=F32)


def kernel(emb_hbm, cot_ref, w_ref, rows_ref, spread_hbm, pick_hbm, mask_hbm, wg_ref, tg_ref,
           emb_ref, spread_ref, pick_ref, mask_ref,
           cot_v, cz_v, w_v, ei, items, pairs_v, pt_v, pg_v, pos_v, vals_v, meta_v,
           hot_v, hotx_v, wp_f, wp_s, wp_r, ws_s, ws_r, wl_s, wl_r, send_v, recv_v, x_v,
           loc_sem, ag_ss, ag_rs, cz_ss, cz_rs, pt_ss, pt_rs, wp_ss, wp_rs, ws_ss, ws_rs, wl_ss, wl_rs,
           a_ss, a_rs, x_ss, x_rs):
    me_s = lax.axis_index("set")
    me_d = lax.axis_index("dp")
    x, yl = me_s // 2, me_s % 2
    right = ((x + 1) % 4) * 2 + yl
    left = ((x + 3) % 4) * 2 + yl
    opp = ((x + 2) % 4) * 2 + yl
    over = me_s + 1 - 2 * yl
    right_o = right + 1 - 2 * yl
    left_o = left + 1 - 2 * yl
    opp_o = opp + 1 - 2 * yl
    z, yh, core = me_d // 4, (me_d // 2) % 2, me_d % 2
    twin = me_d + 1 - 2 * core
    y_part = me_d + 2 - 4 * yh
    unit = me_d % 4

    def rcopy(src, dst, ss, rs, **where):
        return pltpu.make_async_remote_copy(
            src_ref=src, dst_ref=dst, send_sem=ss, recv_sem=rs, device_id=where, device_id_type=MESH)

    own_copies = []
    for h in range(2):
        for cc in range(2):
            own_copies.append(pltpu.make_async_copy(
                cot_ref.at[:, pl.ds((h * 2 + cc) * 256, 256)], cot_v.at[me_s, cc, h], loc_sem.at[h * 2 + cc]))
    inputs = ((emb_hbm, emb_ref), (pick_hbm, pick_ref), (mask_hbm, mask_ref), (spread_hbm, spread_ref), (w_ref, w_v))
    in_copies = [pltpu.make_async_copy(a, b, loc_sem.at[4 + i]) for i, (a, b) in enumerate(inputs)]
    own_cz = pltpu.make_async_copy(cot_ref.at[:, pl.ds(pl.multiple_of(z * 128, 128), 128)],
                                   cz_v.at[me_s, z // 4, z % 4], loc_sem.at[9])
    for copy in own_copies + [own_cz] + in_copies:
        copy.start()

    barrier = pltpu.get_barrier_semaphore()
    for peer in (right, left, over):
        pl.semaphore_signal(barrier, inc=1, device_id={"set": peer}, device_id_type=MESH)

    def greet(i, carry):
        pl.semaphore_signal(barrier, inc=1, device_id={"dp": (me_d + i) % DP}, device_id_type=MESH)
        return carry

    lax.fori_loop(1, DP, greet, 0)
    for copy in own_copies:
        copy.wait()
    pl.semaphore_wait(barrier, 3 + DP - 1)

    sent = []

    def start(copy):
        copy.start()
        sent.append(copy)

    def settle():
        for copy in sent:
            copy.wait_send()
        sent.clear()

    def ag(g, k, src, peer):
        start(rcopy(src, src, ag_ss.at[g, k], ag_rs.at[g, k], set=peer))

    def ag_wait(g, k, block):
        rcopy(block, block, ag_ss.at[g, k], ag_rs.at[g, k], set=right).wait_recv()

    def ag_own(g, buf):
        ag(g, 0, buf.at[me_s, 0], right)
        ag(g, 2, buf.at[me_s, 1], left)
        ag(g, 4, buf.at[me_s], over)
        ag(g, 1, buf.at[me_s, 1], right)
        ag(g, 3, buf.at[me_s, 0], left)

    def ag_halves(g, buf):
        ag_wait(g, 0, buf.at[left, 0])
        ag(g, 5, buf.at[left, 0], right)
        ag_wait(g, 2, buf.at[right, 1])
        ag(g, 6, buf.at[right, 1], left)

    def ag_over(g, buf):
        ag_wait(g, 4, buf.at[over])
        ag(g, 7, buf.at[over], right)
        ag(g, 8, buf.at[over], left)

    def ag_near(g, buf):
        ag_wait(g, 1, buf.at[left, 1])
        ag_wait(g, 3, buf.at[right, 0])

    def ag_opp(g, buf):
        ag_wait(g, 5, buf.at[opp, 0])
        if g == 0:
            ag(g, 9, buf.at[opp, 0], over)
        ag_wait(g, 6, buf.at[opp, 1])
        if g == 0:
            ag(g, 10, buf.at[opp, 1], over)

    def ag_opp_o(g, buf):
        ag_wait(g, 9, buf.at[opp_o, 0])
        ag_wait(g, 10, buf.at[opp_o, 1])

    ag_own(0, cot_v)

    def cz_copy(i):
        q = (z + i) % 8
        return rcopy(cot_ref.at[:, pl.ds(pl.multiple_of(q * 128, 128), 128)], cz_v.at[me_s, z // 4, z % 4],
                     cz_ss.at[i], cz_rs.at[z], dp=(me_d + 4 * i) % DP)

    far_first = (4, 3, 5, 2, 6, 1, 7)
    for i in far_first:
        start(cz_copy(i))

    for copy in in_copies[:4]:
        copy.wait()
    lane = lax.broadcasted_iota(jnp.int32, (B, 128), 1)
    for m in range(8):
        a = emb_ref[0, :, m * 128:(m + 1) * 128].astype(F32)
        b = emb_ref[1, :, m * 128:(m + 1) * 128].astype(F32)
        ei[2 * m] = jnp.where(lane < 64, a, pltpu.roll(b, 64, 1)).astype(BF)
        ei[2 * m + 1] = jnp.where(lane < 64, pltpu.roll(a, 64, 1), b).astype(BF)

    def diagonal():
        r = lax.broadcasted_iota(jnp.int32, (256, 256), 0)
        c = lax.broadcasted_iota(jnp.int32, (256, 256), 1)
        return (r % 16) == (c % 16)

    def group_rows(g):
        return pl.ds(pl.multiple_of(g * 16, 16), 16)

    def pair_step(g, carry):
        eg = ei[:, group_rows(g), :].reshape(256, 128)
        lane_g = lax.broadcasted_iota(jnp.int32, (256, 128), 1)
        for s in range(2):
            half = jnp.where((lane_g < 64) == (s == 0), eg.astype(F32), 0.0).astype(BF)
            gram = jnp.where(diagonal(), dot_nt(half, eg), 0.0).astype(BF)
            picked = dot(gram, pick_ref[...]) * mask_ref[:, :128].astype(F32)
            pairs_v[group_rows(g), s * 128:(s + 1) * 128] = jnp.sum(picked.reshape(F, 16, 128), axis=0)
        return carry

    lax.fori_loop(0, 4, pair_step, 0)

    ag_halves(0, cot_v)
    lax.fori_loop(4, 8, pair_step, 0)
    turned = pairs_v[...].T
    own_pairs = pl.ds(pl.multiple_of(z * B, B), B)
    pt_v[:, own_pairs] = jnp.concatenate([turned[:PAIRS], turned[128:128 + PAIRS]], axis=0).astype(BF)

    def pt_copy(i):
        return rcopy(pt_v.at[:, own_pairs], pt_v.at[:, own_pairs], pt_ss.at[i], pt_rs.at[z], dp=(me_d + 4 * i) % DP)

    for i in far_first:
        start(pt_copy(i))

    ag_over(0, cot_v)
    ag_near(0, cot_v)

    in_copies[4].wait()
    pg_v[...] = jnp.zeros_like(pg_v)

    def pg_add(j):
        total = None
        for h in range(2):
            for cc in range(2):
                cols = pl.ds(pl.multiple_of(j * 1024 + (h * 2 + cc) * 256, 256), 256)
                term = dot_nt(cot_v[j, cc, h], w_v[:, cols])
                total = term if total is None else total + term
        pg_v[:, :2 * PAIRS] += total

    def wp_copy(j, i):
        to = (unit + i) % 4
        return rcopy(wp_s.at[j, pl.ds(pl.multiple_of(to * 64, 64), 64)], wp_r.at[j, unit],
                     wp_ss.at[j, i], wp_rs.at[j, unit], dp=z * 4 + to)

    def wp_make(j):
        value = dot(pt_v[...], cz_v[j].reshape(8 * B, 128))
        value = jnp.concatenate([value, jnp.zeros((16, 128), F32)], axis=0)
        wp_f[j] = value
        wp_s[j] = value.astype(BF)
        for i in (2, 3, 1):
            start(wp_copy(j, i))

    def ws_copy(j):
        return rcopy(ws_s.at[j], ws_r.at[z % 2, unit], ws_ss.at[j], ws_rs.at[z % 2, unit], dp=j * 4 + z // 2)

    def ws_make(j):
        total = wp_f[j, pl.ds(pl.multiple_of(unit * 64, 64), 64)]
        for i in (1, 3, 2):
            source = (unit + i) % 4
            rcopy(wp_s.at[j, pl.ds(0, 64)], wp_r.at[j, source], wp_ss.at[j, i], wp_rs.at[j, source], dp=twin).wait_recv()
            total = total + wp_r[j, source].astype(F32)
        block = total.astype(BF)
        ws_s[j] = block
        here = j * 4 + z // 2 == me_d

        @pl.when(here)
        def _():
            ws_r[z % 2, unit] = block

        @pl.when(jnp.logical_not(here))
        def _():
            ws_copy(j).start()

    late = (opp_o, left_o, right_o)
    late_here = (z == opp_o) | (z == left_o) | (z == right_o)

    def wl_copy(t):
        return rcopy(wl_s.at[t], wl_r.at[z % 2, unit], wl_ss.at[t], wl_rs.at[z % 2, unit], dp=late[t] * 4 + z // 2)

    def wl_make(t):
        block = dot(pt_v[...], cz_v[late[t]].reshape(8 * B, 128)).astype(BF)
        wl_s[t] = block
        here = late[t] * 4 + z // 2 == me_d

        @pl.when(here)
        def _():
            wl_r[z % 2, unit] = block

        @pl.when(jnp.logical_not(here))
        def _():
            wl_copy(t).start()

    for j in (me_s, over, left, right):
        pg_add(j)

    ag_opp(0, cot_v)
    own_cz.wait()
    for i in range(1, 8):
        block = cz_v.at[me_s, ((z + i) % 8) // 4, (z + i) % 4]
        rcopy(block, block, cz_ss.at[i], cz_rs.at[(z + i) % 8], dp=twin).wait_recv()
    ag_own(1, cz_v)

    rows_t = rows_ref[...].astype(F32)
    owner = jnp.floor(rows_t * (1.0 / ROWS_DEV))
    local = rows_t - owner * ROWS_DEV
    local_hi = jnp.floor(local * (1.0 / 256))
    g_hi = jnp.floor(rows_t * (1.0 / 128))
    before = (lax.broadcasted_iota(jnp.int32, (128, 128), 0)
              < lax.broadcasted_iota(jnp.int32, (128, 128), 1)).astype(F32).astype(BF)
    owner_id = lax.broadcasted_iota(jnp.int32, (DP, 128), 0).astype(F32)
    seen = jnp.zeros((DP, 1), F32)
    vals_v[...] = jnp.zeros_like(vals_v)
    for f in range(F):
        hot = jnp.where(owner_id == owner[f:f + 1], 1.0, 0.0)
        earlier = dot(hot.astype(BF), before) + seen
        seen = seen + jnp.sum(hot, axis=1, keepdims=True)
        rank = jnp.sum(hot * earlier, axis=0, keepdims=True)
        pos = jnp.where(rank < KEEP, owner[f:f + 1] * 64 + rank, DP * 64 + rank - KEEP)
        pos_v[f:f + 1, :] = pos.astype(jnp.int32)
        cols = slice(f * 128, (f + 1) * 128)
        vals_v[0:1, cols] = local[f:f + 1] - 256 * local_hi[f:f + 1]
        vals_v[1:2, cols] = local_hi[f:f + 1]
        vals_v[2:3, cols] = rows_t[f:f + 1] - 128 * g_hi[f:f + 1]
        vals_v[3:4, cols] = g_hi[f:f + 1]

    def hot_step(k, carry):
        slot = lax.broadcasted_iota(jnp.int32, (256, 128), 0) + k * 256
        for f in range(F):
            hot_v[k, :, f * 128:(f + 1) * 128] = jnp.where(slot == pos_v[f:f + 1, :], 1.0, 0.0).astype(BF)
        ids = dot_nt(vals_v[...].astype(BF), hot_v[k])
        low = lax.broadcasted_iota(jnp.int32, (1, 128), 1) < 64
        for q in range(4):
            cols = slice((q // 2) * 128, (q // 2) * 128 + 128)
            lo, hi = ids[0:1, cols], ids[1:2, cols]
            if q % 2 == 0:
                row = jnp.where(low, lo, pltpu.roll(jnp.broadcast_to(hi, (8, 128)), 64, 1)[0:1])
            else:
                row = jnp.where(low, pltpu.roll(jnp.broadcast_to(lo, (8, 128)), 64, 1)[0:1], hi)
            meta_v[k, q:q + 1, :] = row
        return carry

    pg_add(opp)
    lax.fori_loop(0, 8, hot_step, 0)
    slot_x = lax.broadcasted_iota(jnp.int32, (XROWS, 128), 0) + DP * 64
    for f in range(F):
        hotx_v[:, f * 128:(f + 1) * 128] = jnp.where(slot_x == pos_v[f:f + 1, :], 1.0, 0.0).astype(BF)
    ids_x = dot_nt(vals_v[...].astype(BF), hotx_v[...])
    x_v[:, :, :, XROWS:] = jnp.zeros((2, 2, 8, 128 - XROWS, 128), BF)

    ag_opp_o(0, cot_v)
    pg_add(opp_o)
    ag_wait(0, 7, cot_v.at[left_o])
    ag_wait(0, 8, cot_v.at[right_o])
    pg_add(left_o)
    pg_add(right_o)

    pg_all = pg_v[...]
    pg_v[...] = pg_all.astype(BF).astype(F32)

    def emb_step(g, carry):
        eg = ei[:, group_rows(g), :].reshape(256, 128)
        a = pg_v[group_rows(g), :]
        grads = []
        for s in range(2):
            one = (a if s == 0 else pltpu.roll(a, 256 - PAIRS, 1))[:, :128]
            both = jnp.concatenate([one, one], axis=1).astype(BF)
            tall = jnp.concatenate([both] * F, axis=0) * mask_ref[...]
            sym = jnp.where(diagonal(), dot(tall, spread_ref[...]), 0.0).astype(BF)
            grads.append(dot(sym, eg))
        lane_g = lax.broadcasted_iota(jnp.int32, (256, 128), 1)
        items[:, group_rows(g), :] = jnp.where(lane_g < 64, grads[0], grads[1]).astype(BF).reshape(F, 16, 128)
        return carry

    lax.fori_loop(0, 2, emb_step, 0, unroll=2)
    ag_halves(1, cz_v)
    lax.fori_loop(2, 8, emb_step, 0, unroll=3)
    ag_over(1, cz_v)
    for i in range(1, 8):
        block = pt_v.at[:, pl.ds(pl.multiple_of((z + i) % 8 * B, B), B)]
        rcopy(block, block, pt_ss.at[i], pt_rs.at[(z + i) % 8], dp=twin).wait_recv()
    wp_make(me_s)

    x_tile = dot(hotx_v[...], items[...].reshape(B * F, 128))
    row_x = lax.broadcasted_iota(jnp.int32, (XROWS, 128), 0)
    ids_x = jnp.concatenate([ids_x, jnp.zeros((ids_x.shape[0], 128 - XROWS), F32)], axis=1)
    x_tile = jnp.where(row_x == 66, ids_x[2:3], jnp.where(row_x == 67, ids_x[3:4], x_tile))
    x_v[core, yh, z, :XROWS] = x_tile.astype(BF)
    x_own = x_v.at[core, yh, z, pl.ds(0, XROWS)]

    def x_copy(i):
        return rcopy(x_own, x_own, x_ss.at[i], x_rs.at[z], dp=(me_d + 4 * i) % DP)

    for i in far_first:
        start(x_copy(i))

    def a_copy(o):
        return rcopy(send_v.at[o], recv_v.at[me_d], a_ss.at[o], a_rs.at[me_d], dp=o)

    def turn(i):
        return 4 + (2 * (i % 2) - 1) * ((i + 1) // 2)

    def a_step(i, carry):
        k = (z + turn(i)) % 8
        tile = dot(hot_v[k], items[...].reshape(B * F, 128))
        row = lax.broadcasted_iota(jnp.int32, (64, 128), 0)
        for q in range(4):
            o = k * 4 + q
            block = jnp.where(row == KEEP, meta_v[k, q:q + 1, :], tile[q * 64:(q + 1) * 64]).astype(BF)
            send_v[o] = block

            @pl.when(o == me_d)
            def _():
                recv_v[o] = block

            @pl.when(o != me_d)
            def _():
                a_copy(o).start()
        return carry

    lax.fori_loop(0, 2, a_step, 0)
    ag_near(1, cz_v)
    for j in (over, left, right):
        wp_make(j)
    lax.fori_loop(2, 5, a_step, 0)
    ag_opp(1, cz_v)
    wp_make(opp)
    lax.fori_loop(5, 8, a_step, 0)

    ws_make(me_s)
    for j in (over, left, right):
        ws_make(j)

    tg_ref[...] = jnp.zeros_like(tg_ref)
    row_id = lax.broadcasted_iota(jnp.int32, (ROWS_DEV, 128), 0).astype(F32)

    def a_add(i, carry):
        k = (z + 8 - turn(i)) % 8
        low = lax.broadcasted_iota(jnp.int32, (8, 128), 1) < 64
        dead = lax.broadcasted_iota(jnp.int32, (8, 128), 1) % 64 >= KEEP
        for q in range(4):
            @pl.when(k * 4 + q != me_d)
            def _():
                rcopy(send_v.at[me_d], recv_v.at[k * 4 + q], a_ss.at[me_d], a_rs.at[k * 4 + q], dp=twin).wait_recv()
        ids = []
        for q in range(4):
            got = jnp.broadcast_to(recv_v[k * 4 + q, KEEP:KEEP + 1, :].astype(F32), (8, 128))
            swapped = pltpu.roll(got, 64, 1)
            ids.append(got + 256 * swapped if q % 2 == 0 else swapped + 256 * got)
        hots = []
        for m in range(2):
            both = jnp.where(dead, -1.0, jnp.where(low, ids[2 * m], ids[2 * m + 1]))[0:1]
            hots.append(jnp.where(row_id == both, 1.0, 0.0).astype(BF))
        values = recv_v[pl.ds(pl.multiple_of(k * 4, 4), 4)].reshape(256, 128)
        tg_ref[...] += dot(jnp.concatenate(hots, axis=1), values)
        return carry

    for i in range(1, 8):
        block = x_v.at[core, yh, (z + 8 - i) % 8, pl.ds(0, XROWS)]
        rcopy(block, block, x_ss.at[0], x_rs.at[(z + 8 - i) % 8], dp=twin).wait_recv()
    x_half = x_v.at[core, yh, :, pl.ds(0, XROWS)]
    start(rcopy(x_half, x_half, x_ss.at[8], x_rs.at[8], dp=y_part))

    ag_wait(1, 7, cz_v.at[left_o])
    ag(1, 9, cz_v.at[left_o, 0], right)
    ag_wait(1, 8, cz_v.at[right_o])
    ag(1, 10, cz_v.at[right_o, 1], left)
    wl_make(1)
    wl_make(2)
    ag_opp_o(1, cz_v)
    wl_make(0)
    settle()
    ws_make(opp)
    lax.fori_loop(0, 4, a_add, 0)

    other = x_v.at[core, 1 - yh, :, pl.ds(0, XROWS)]
    rcopy(other, other, x_ss.at[8], x_rs.at[8], dp=y_part).wait_recv()
    x_all = x_v.at[core, :, :, pl.ds(0, XROWS)]
    start(rcopy(x_all, x_all, x_ss.at[9], x_rs.at[9], dp=twin))

    lax.fori_loop(4, 8, a_add, 0)

    base = (me_d * ROWS_DEV).astype(F32)
    live = lax.broadcasted_iota(jnp.int32, (1, 128), 1) < 66

    def x_add(cc):
        def body(i, carry):
            half, first = i // 2, (i % 2) * 4
            hots = []
            for q in range(4):
                low = x_v[cc, half, first + q, 66:67, :].astype(F32)
                high = x_v[cc, half, first + q, 67:68, :].astype(F32)
                ids = jnp.where(live, low + 128 * high - base, -1.0)
                hots.append(jnp.where(row_id == ids, 1.0, 0.0).astype(BF))
            values = x_v[cc, half, pl.ds(pl.multiple_of(first, 4), 4)].reshape(512, 128)
            tg_ref[...] += dot(jnp.concatenate(hots, axis=1), values)
            return carry

        lax.fori_loop(0, 4, body, 0)

    x_add(core)
    x_twin = x_v.at[1 - core, :, :, pl.ds(0, XROWS)]
    rcopy(x_twin, x_twin, x_ss.at[9], x_rs.at[9], dp=twin).wait_recv()
    x_add(1 - core)

    def drain(i, carry):
        a_copy((me_d + i) % DP).wait_send()
        return carry

    lax.fori_loop(1, DP, drain, 0)

    def from_line(half, source, block, arrived):
        @pl.when((unit * 2 + half) * 4 + source != me_d)
        def _():
            rcopy(block, block, ws_ss.at[0], arrived, dp=twin).wait_recv()

    @pl.when(late_here)
    def _():
        for half in range(2):
            total = None
            for source in range(4):
                from_line(half, source, wl_r.at[half, source], wl_rs.at[half, source])
                term = wl_r[half, source].astype(F32)
                total = term if total is None else total + term
            wg_ref[:, half * 128:(half + 1) * 128] = total.astype(BF)

    @pl.when(jnp.logical_not(late_here))
    def _():
        for half in range(2):
            for source in range(4):
                from_line(half, source, ws_r.at[half, source], ws_rs.at[half, source])
                rows = min(64, 2 * PAIRS - source * 64)
                wg_ref[source * 64:source * 64 + rows, half * 128:(half + 1) * 128] = ws_r[half, source, :rows]

    settle()
    for j in (me_s, over, left, right, opp):
        @pl.when(j * 4 + z // 2 != me_d)
        def _():
            ws_copy(j).wait_send()
    for t in range(3):
        @pl.when(late[t] * 4 + z // 2 != me_d)
        def _():
            wl_copy(t).wait_send()


def hand_over(wg_in, tg_in, wg_out, tg_out):
    wg_out[...] = wg_in[...]
    tg_out[...] = tg_in[...]


def on_device(embeddings, cotangent, first_weight, feature_rows):
    vmem = pl.BlockSpec(memory_space=pltpu.VMEM)
    hbm = pl.BlockSpec(memory_space=pl.ANY)
    dma = pltpu.SemaphoreType.DMA
    consts = [jnp.asarray(a) for a in constants()]
    shapes = (jax.ShapeDtypeStruct((2 * PAIRS, 256), BF), jax.ShapeDtypeStruct((ROWS_DEV, 128), F32))
    results = pl.pallas_call(
        kernel,
        out_shape=(pltpu.VMEM((2 * PAIRS, 256), BF), pltpu.VMEM((ROWS_DEV, 128), F32)),
        in_specs=[hbm, hbm, hbm, vmem, hbm, hbm, hbm],
        out_specs=(vmem, vmem),
        scratch_shapes=[
            pltpu.VMEM((2, B, 1024), BF),
            pltpu.VMEM((256, 256), BF),
            pltpu.VMEM((256, 128), BF),
            pltpu.VMEM((256, 256), BF),
            pltpu.VMEM((8, 2, 2, B, 256), BF),
            pltpu.VMEM((8, 2, 4, B, 128), BF),
            pltpu.VMEM((2 * PAIRS, 8192), BF),
            pltpu.VMEM((F, B, 128), BF),
            pltpu.VMEM((F, B, 128), BF),
            pltpu.VMEM((B, 256), F32),
            pltpu.VMEM((2 * PAIRS, 8 * B), BF),
            pltpu.VMEM((B, 256), F32),
            pltpu.VMEM((F, 128), jnp.int32),
            pltpu.VMEM((16, B * F), F32),
            pltpu.VMEM((8, 8, 128), F32),
            pltpu.VMEM((8, 256, B * F), BF),
            pltpu.VMEM((XROWS, B * F), BF),
            pltpu.VMEM((8, 256, 128), F32),
            pltpu.VMEM((8, 256, 128), BF),
            pltpu.VMEM((8, 4, 64, 128), BF),
            pltpu.VMEM((8, 64, 128), BF),
            pltpu.VMEM((2, 4, 64, 128), BF),
            pltpu.VMEM((3, 2 * PAIRS, 128), BF),
            pltpu.VMEM((2, 4, 2 * PAIRS, 128), BF),
            pltpu.VMEM((DP, 64, 128), BF),
            pltpu.VMEM((DP, 64, 128), BF),
            pltpu.VMEM((2, 2, 8, 128, 128), BF),
            dma((10,)), dma((2, 11)), dma((2, 11)), dma((8,)), dma((8,)), dma((8,)), dma((8,)),
            dma((8, 4)), dma((8, 4)), dma((8,)), dma((2, 4)), dma((3,)), dma((2, 4)),
            dma((DP,)), dma((DP,)), dma((10,)), dma((10,)),
        ],
        compiler_params=pltpu.CompilerParams(
            collective_id=0, has_side_effects=True, vmem_limit_bytes=56 * 1024 * 1024),
    )(embeddings, cotangent, first_weight, feature_rows.T, *consts)
    return pl.pallas_call(
        hand_over,
        out_shape=shapes,
        in_specs=[vmem, vmem],
        out_specs=(vmem, vmem),
    )(*[pltpu.with_memory_space_constraint(r, pltpu.VMEM) for r in results])


def solution(mesh):
    return jax.shard_map(
        on_device,
        mesh=mesh,
        in_specs=(P("set", "dp", None), P("dp", "set"), P("set", None), P("dp", None)),
        out_specs=(P("set", "dp"), P("dp", "set")),
        check_vma=False,
    )
```

```python
import functools

import jax
import jax.numpy as jnp
import numpy as np
from jax import lax
from jax.experimental import pallas as pl
from jax.experimental.pallas import tpu as pltpu
from jax.sharding import PartitionSpec as P

K = 64
F = 16
ROWS_DEV = 512
PAIRS = 120
B = 128
KEEP = 62
XROWS = 80
DP = 32
BF = jnp.bfloat16
F32 = jnp.float32
MESH = pl.DeviceIdType.MESH


def constants():
    first, second = np.triu_indices(F, 1)
    spread = np.zeros((256, F, 16), np.float32)
    mask = np.zeros((F, 16, 256), np.float32)
    for p in range(PAIRS):
        spread[p, second[p], :] = 1
        spread[128 + p, first[p], :] = 1
        mask[first[p], :, p] = 1
        mask[second[p], :, 128 + p] = 1
    spread = spread.reshape(256, 256)
    pick = np.ascontiguousarray(spread[:128].T)
    return [a.astype(BF) for a in (spread, pick, mask.reshape(256, 256))]


def dot(a, b):
    return jnp.dot(a, b, preferred_element_type=F32)


def dot_nt(a, b):
    return lax.dot_general(a, b, (((1,), (1,)), ((), ())), preferred_element_type=F32)


def kernel(emb_hbm, cot_ref, w_ref, rows_ref, spread_hbm, pick_hbm, mask_hbm, wg_ref, tg_ref,
           emb_ref, spread_ref, pick_ref, mask_ref,
           cot_v, cz_v, w_v, ei, items, pairs_v, pt_v, pg_v, pos_v, vals_v, meta_v,
           hot_v, hotx_v, wp_f, wp_s, wp_r, ws_s, ws_r, wl_s, wl_r, send_v, recv_v, x_v,
           loc_sem, ag_ss, ag_rs, cz_ss, cz_rs, pt_ss, pt_rs, wp_ss, wp_rs, ws_ss, ws_rs, wl_ss, wl_rs,
           a_ss, a_rs, x_ss, x_rs):
    me_s = lax.axis_index("set")
    me_d = lax.axis_index("dp")
    x, yl = me_s // 2, me_s % 2
    right = ((x + 1) % 4) * 2 + yl
    left = ((x + 3) % 4) * 2 + yl
    opp = ((x + 2) % 4) * 2 + yl
    over = me_s + 1 - 2 * yl
    right_o = right + 1 - 2 * yl
    left_o = left + 1 - 2 * yl
    opp_o = opp + 1 - 2 * yl
    z, yh, core = me_d // 4, (me_d // 2) % 2, me_d % 2
    twin = me_d + 1 - 2 * core
    y_part = me_d + 2 - 4 * yh
    unit = me_d % 4

    def rcopy(src, dst, ss, rs, **where):
        return pltpu.make_async_remote_copy(
            src_ref=src, dst_ref=dst, send_sem=ss, recv_sem=rs, device_id=where, device_id_type=MESH)

    own_copies = []
    for h in range(2):
        for cc in range(2):
            own_copies.append(pltpu.make_async_copy(
                cot_ref.at[:, pl.ds((h * 2 + cc) * 256, 256)], cot_v.at[me_s, cc, h], loc_sem.at[h * 2 + cc]))
    inputs = ((emb_hbm, emb_ref), (pick_hbm, pick_ref), (mask_hbm, mask_ref), (spread_hbm, spread_ref), (w_ref, w_v))
    in_copies = [pltpu.make_async_copy(a, b, loc_sem.at[4 + i]) for i, (a, b) in enumerate(inputs)]
    own_cz = pltpu.make_async_copy(cot_ref.at[:, pl.ds(pl.multiple_of(z * 128, 128), 128)],
                                   cz_v.at[me_s, z // 4, z % 4], loc_sem.at[9])
    for copy in own_copies + [own_cz] + in_copies:
        copy.start()

    barrier = pltpu.get_barrier_semaphore()
    for peer in (right, left, over):
        pl.semaphore_signal(barrier, inc=1, device_id={"set": peer}, device_id_type=MESH)

    def greet(i, carry):
        pl.semaphore_signal(barrier, inc=1, device_id={"dp": (me_d + i) % DP}, device_id_type=MESH)
        return carry

    lax.fori_loop(1, DP, greet, 0)
    for copy in own_copies:
        copy.wait()
    pl.semaphore_wait(barrier, 3 + DP - 1)

    sent = []

    def start(copy):
        copy.start()
        sent.append(copy)

    def settle():
        for copy in sent:
            copy.wait_send()
        sent.clear()

    def ag(g, k, src, peer):
        start(rcopy(src, src, ag_ss.at[g, k], ag_rs.at[g, k], set=peer))

    def ag_wait(g, k, block):
        rcopy(block, block, ag_ss.at[g, k], ag_rs.at[g, k], set=right).wait_recv()

    def ag_own(g, buf):
        ag(g, 0, buf.at[me_s, 0], right)
        ag(g, 2, buf.at[me_s, 1], left)
        ag(g, 4, buf.at[me_s], over)
        ag(g, 1, buf.at[me_s, 1], right)
        ag(g, 3, buf.at[me_s, 0], left)

    def ag_halves(g, buf):
        ag_wait(g, 0, buf.at[left, 0])
        ag(g, 5, buf.at[left, 0], right)
        ag_wait(g, 2, buf.at[right, 1])
        ag(g, 6, buf.at[right, 1], left)

    def ag_over(g, buf):
        ag_wait(g, 4, buf.at[over])
        ag(g, 7, buf.at[over], right)
        ag(g, 8, buf.at[over], left)

    def ag_near(g, buf):
        ag_wait(g, 1, buf.at[left, 1])
        ag_wait(g, 3, buf.at[right, 0])

    def ag_opp(g, buf):
        ag_wait(g, 5, buf.at[opp, 0])
        if g == 0:
            ag(g, 9, buf.at[opp, 0], over)
        ag_wait(g, 6, buf.at[opp, 1])
        if g == 0:
            ag(g, 10, buf.at[opp, 1], over)

    def ag_opp_o(g, buf):
        ag_wait(g, 9, buf.at[opp_o, 0])
        ag_wait(g, 10, buf.at[opp_o, 1])

    ag_own(0, cot_v)

    def cz_copy(i):
        q = (z + i) % 8
        return rcopy(cot_ref.at[:, pl.ds(pl.multiple_of(q * 128, 128), 128)], cz_v.at[me_s, z // 4, z % 4],
                     cz_ss.at[i], cz_rs.at[z], dp=(me_d + 4 * i) % DP)

    far_first = (4, 3, 5, 2, 6, 1, 7)
    for i in far_first:
        start(cz_copy(i))

    for copy in in_copies[:4]:
        copy.wait()
    lane = lax.broadcasted_iota(jnp.int32, (B, 128), 1)
    for m in range(8):
        a = emb_ref[0, :, m * 128:(m + 1) * 128].astype(F32)
        b = emb_ref[1, :, m * 128:(m + 1) * 128].astype(F32)
        ei[2 * m] = jnp.where(lane < 64, a, pltpu.roll(b, 64, 1)).astype(BF)
        ei[2 * m + 1] = jnp.where(lane < 64, pltpu.roll(a, 64, 1), b).astype(BF)

    def diagonal():
        r = lax.broadcasted_iota(jnp.int32, (256, 256), 0)
        c = lax.broadcasted_iota(jnp.int32, (256, 256), 1)
        return (r % 16) == (c % 16)

    def group_rows(g):
        return pl.ds(pl.multiple_of(g * 16, 16), 16)

    def pair_step(g, carry):
        eg = ei[:, group_rows(g), :].reshape(256, 128)
        lane_g = lax.broadcasted_iota(jnp.int32, (256, 128), 1)
        for s in range(2):
            half = jnp.where((lane_g < 64) == (s == 0), eg.astype(F32), 0.0).astype(BF)
            gram = jnp.where(diagonal(), dot_nt(half, eg), 0.0).astype(BF)
            picked = dot(gram, pick_ref[...]) * mask_ref[:, :128].astype(F32)
            pairs_v[group_rows(g), s * 128:(s + 1) * 128] = jnp.sum(picked.reshape(F, 16, 128), axis=0)
        return carry

    lax.fori_loop(0, 4, pair_step, 0)

    ag_halves(0, cot_v)
    lax.fori_loop(4, 8, pair_step, 0)
    turned = pairs_v[...].T
    own_pairs = pl.ds(pl.multiple_of(z * B, B), B)
    pt_v[:, own_pairs] = jnp.concatenate([turned[:PAIRS], turned[128:128 + PAIRS]], axis=0).astype(BF)

    def pt_copy(i):
        return rcopy(pt_v.at[:, own_pairs], pt_v.at[:, own_pairs], pt_ss.at[i], pt_rs.at[z], dp=(me_d + 4 * i) % DP)

    for i in far_first:
        start(pt_copy(i))

    ag_over(0, cot_v)
    ag_near(0, cot_v)

    in_copies[4].wait()
    pg_v[...] = jnp.zeros_like(pg_v)

    def pg_add(j):
        total = None
        for h in range(2):
            for cc in range(2):
                cols = pl.ds(pl.multiple_of(j * 1024 + (h * 2 + cc) * 256, 256), 256)
                term = dot_nt(cot_v[j, cc, h], w_v[:, cols])
                total = term if total is None else total + term
        pg_v[:, :2 * PAIRS] += total

    def wp_copy(j, i):
        to = (unit + i) % 4
        return rcopy(wp_s.at[j, pl.ds(pl.multiple_of(to * 64, 64), 64)], wp_r.at[j, unit],
                     wp_ss.at[j, i], wp_rs.at[j, unit], dp=z * 4 + to)

    def wp_make(j):
        value = dot(pt_v[...], cz_v[j].reshape(8 * B, 128))
        value = jnp.concatenate([value, jnp.zeros((16, 128), F32)], axis=0)
        wp_f[j] = value
        wp_s[j] = value.astype(BF)
        for i in (2, 3, 1):
            start(wp_copy(j, i))

    def ws_copy(j):
        return rcopy(ws_s.at[j], ws_r.at[z % 2, unit], ws_ss.at[j], ws_rs.at[z % 2, unit], dp=j * 4 + z // 2)

    def ws_make(j):
        total = wp_f[j, pl.ds(pl.multiple_of(unit * 64, 64), 64)]
        for i in (1, 3, 2):
            source = (unit + i) % 4
            rcopy(wp_s.at[j, pl.ds(0, 64)], wp_r.at[j, source], wp_ss.at[j, i], wp_rs.at[j, source], dp=twin).wait_recv()
            total = total + wp_r[j, source].astype(F32)
        block = total.astype(BF)
        ws_s[j] = block
        here = j * 4 + z // 2 == me_d

        @pl.when(here)
        def _():
            ws_r[z % 2, unit] = block

        @pl.when(jnp.logical_not(here))
        def _():
            ws_copy(j).start()

    late = (opp_o, left_o, right_o)
    late_here = (z == opp_o) | (z == left_o) | (z == right_o)

    def wl_copy(t):
        return rcopy(wl_s.at[t], wl_r.at[z % 2, unit], wl_ss.at[t], wl_rs.at[z % 2, unit], dp=late[t] * 4 + z // 2)

    def wl_make(t):
        block = dot(pt_v[...], cz_v[late[t]].reshape(8 * B, 128)).astype(BF)
        wl_s[t] = block
        here = late[t] * 4 + z // 2 == me_d

        @pl.when(here)
        def _():
            wl_r[z % 2, unit] = block

        @pl.when(jnp.logical_not(here))
        def _():
            wl_copy(t).start()

    for j in (me_s, over, left, right):
        pg_add(j)

    ag_opp(0, cot_v)
    own_cz.wait()
    for i in range(1, 8):
        block = cz_v.at[me_s, ((z + i) % 8) // 4, (z + i) % 4]
        rcopy(block, block, cz_ss.at[i], cz_rs.at[(z + i) % 8], dp=twin).wait_recv()
    ag_own(1, cz_v)

    rows_t = rows_ref[...].astype(F32)
    owner = jnp.floor(rows_t * (1.0 / ROWS_DEV))
    local = rows_t - owner * ROWS_DEV
    local_hi = jnp.floor(local * (1.0 / 256))
    g_hi = jnp.floor(rows_t * (1.0 / 128))
    before = (lax.broadcasted_iota(jnp.int32, (128, 128), 0)
              < lax.broadcasted_iota(jnp.int32, (128, 128), 1)).astype(F32).astype(BF)
    owner_id = lax.broadcasted_iota(jnp.int32, (DP, 128), 0).astype(F32)
    seen = jnp.zeros((DP, 1), F32)
    vals_v[...] = jnp.zeros_like(vals_v)
    for f in range(F):
        hot = jnp.where(owner_id == owner[f:f + 1], 1.0, 0.0)
        earlier = dot(hot.astype(BF), before) + seen
        seen = seen + jnp.sum(hot, axis=1, keepdims=True)
        rank = jnp.sum(hot * earlier, axis=0, keepdims=True)
        pos = jnp.where(rank < KEEP, owner[f:f + 1] * 64 + rank, DP * 64 + rank - KEEP)
        pos_v[f:f + 1, :] = pos.astype(jnp.int32)
        cols = slice(f * 128, (f + 1) * 128)
        vals_v[0:1, cols] = local[f:f + 1] - 256 * local_hi[f:f + 1]
        vals_v[1:2, cols] = local_hi[f:f + 1]
        vals_v[2:3, cols] = rows_t[f:f + 1] - 128 * g_hi[f:f + 1]
        vals_v[3:4, cols] = g_hi[f:f + 1]

    def hot_step(k, carry):
        slot = lax.broadcasted_iota(jnp.int32, (256, 128), 0) + k * 256
        for f in range(F):
            hot_v[k, :, f * 128:(f + 1) * 128] = jnp.where(slot == pos_v[f:f + 1, :], 1.0, 0.0).astype(BF)
        ids = dot_nt(vals_v[...].astype(BF), hot_v[k])
        low = lax.broadcasted_iota(jnp.int32, (1, 128), 1) < 64
        for q in range(4):
            cols = slice((q // 2) * 128, (q // 2) * 128 + 128)
            lo, hi = ids[0:1, cols], ids[1:2, cols]
            if q % 2 == 0:
                row = jnp.where(low, lo, pltpu.roll(jnp.broadcast_to(hi, (8, 128)), 64, 1)[0:1])
            else:
                row = jnp.where(low, pltpu.roll(jnp.broadcast_to(lo, (8, 128)), 64, 1)[0:1], hi)
            meta_v[k, q:q + 1, :] = row
        return carry

    pg_add(opp)
    lax.fori_loop(0, 8, hot_step, 0)
    slot_x = lax.broadcasted_iota(jnp.int32, (XROWS, 128), 0) + DP * 64
    for f in range(F):
        hotx_v[:, f * 128:(f + 1) * 128] = jnp.where(slot_x == pos_v[f:f + 1, :], 1.0, 0.0).astype(BF)
    ids_x = dot_nt(vals_v[...].astype(BF), hotx_v[...])
    x_v[:, :, :, XROWS:] = jnp.zeros((2, 2, 8, 128 - XROWS, 128), BF)

    ag_opp_o(0, cot_v)
    pg_add(opp_o)
    ag_wait(0, 7, cot_v.at[left_o])
    ag_wait(0, 8, cot_v.at[right_o])
    pg_add(left_o)
    pg_add(right_o)

    pg_all = pg_v[...]
    pg_v[...] = pg_all.astype(BF).astype(F32)

    def emb_step(g, carry):
        eg = ei[:, group_rows(g), :].reshape(256, 128)
        a = pg_v[group_rows(g), :]
        grads = []
        for s in range(2):
            one = (a if s == 0 else pltpu.roll(a, 256 - PAIRS, 1))[:, :128]
            both = jnp.concatenate([one, one], axis=1).astype(BF)
            tall = jnp.concatenate([both] * F, axis=0) * mask_ref[...]
            sym = jnp.where(diagonal(), dot(tall, spread_ref[...]), 0.0).astype(BF)
            grads.append(dot(sym, eg))
        lane_g = lax.broadcasted_iota(jnp.int32, (256, 128), 1)
        items[:, group_rows(g), :] = jnp.where(lane_g < 64, grads[0], grads[1]).astype(BF).reshape(F, 16, 128)
        return carry

    lax.fori_loop(0, 2, emb_step, 0, unroll=2)
    ag_halves(1, cz_v)
    lax.fori_loop(2, 8, emb_step, 0, unroll=3)
    ag_over(1, cz_v)
    for i in range(1, 8):
        block = pt_v.at[:, pl.ds(pl.multiple_of((z + i) % 8 * B, B), B)]
        rcopy(block, block, pt_ss.at[i], pt_rs.at[(z + i) % 8], dp=twin).wait_recv()
    wp_make(me_s)

    x_tile = dot(hotx_v[...], items[...].reshape(B * F, 128))
    row_x = lax.broadcasted_iota(jnp.int32, (XROWS, 128), 0)
    ids_x = jnp.concatenate([ids_x, jnp.zeros((ids_x.shape[0], 128 - XROWS), F32)], axis=1)
    x_tile = jnp.where(row_x == 66, ids_x[2:3], jnp.where(row_x == 67, ids_x[3:4], x_tile))
    x_v[core, yh, z, :XROWS] = x_tile.astype(BF)
    x_own = x_v.at[core, yh, z, pl.ds(0, XROWS)]

    def x_copy(i):
        return rcopy(x_own, x_own, x_ss.at[i], x_rs.at[z], dp=(me_d + 4 * i) % DP)

    for i in far_first:
        start(x_copy(i))

    def a_copy(o):
        return rcopy(send_v.at[o], recv_v.at[me_d], a_ss.at[o], a_rs.at[me_d], dp=o)

    def turn(i):
        return 4 + (2 * (i % 2) - 1) * ((i + 1) // 2)

    def a_step(i, carry):
        k = (z + turn(i)) % 8
        tile = dot(hot_v[k], items[...].reshape(B * F, 128))
        row = lax.broadcasted_iota(jnp.int32, (64, 128), 0)
        for q in range(4):
            o = k * 4 + q
            block = jnp.where(row == KEEP, meta_v[k, q:q + 1, :], tile[q * 64:(q + 1) * 64]).astype(BF)
            send_v[o] = block

            @pl.when(o == me_d)
            def _():
                recv_v[o] = block

            @pl.when(o != me_d)
            def _():
                a_copy(o).start()
        return carry

    lax.fori_loop(0, 2, a_step, 0)
    ag_near(1, cz_v)
    for j in (over, left, right):
        wp_make(j)
    lax.fori_loop(2, 5, a_step, 0)
    ag_opp(1, cz_v)
    wp_make(opp)
    lax.fori_loop(5, 8, a_step, 0)

    ws_make(me_s)
    for j in (over, left, right):
        ws_make(j)

    tg_ref[...] = jnp.zeros_like(tg_ref)
    row_id = lax.broadcasted_iota(jnp.int32, (ROWS_DEV, 128), 0).astype(F32)

    def a_add(i, carry):
        k = (z + 8 - turn(i)) % 8
        low = lax.broadcasted_iota(jnp.int32, (8, 128), 1) < 64
        dead = lax.broadcasted_iota(jnp.int32, (8, 128), 1) % 64 >= KEEP
        for q in range(4):
            @pl.when(k * 4 + q != me_d)
            def _():
                rcopy(send_v.at[me_d], recv_v.at[k * 4 + q], a_ss.at[me_d], a_rs.at[k * 4 + q], dp=twin).wait_recv()
        ids = []
        for q in range(4):
            got = jnp.broadcast_to(recv_v[k * 4 + q, KEEP:KEEP + 1, :].astype(F32), (8, 128))
            swapped = pltpu.roll(got, 64, 1)
            ids.append(got + 256 * swapped if q % 2 == 0 else swapped + 256 * got)
        hots = []
        for m in range(2):
            both = jnp.where(dead, -1.0, jnp.where(low, ids[2 * m], ids[2 * m + 1]))[0:1]
            hots.append(jnp.where(row_id == both, 1.0, 0.0).astype(BF))
        values = recv_v[pl.ds(pl.multiple_of(k * 4, 4), 4)].reshape(256, 128)
        tg_ref[...] += dot(jnp.concatenate(hots, axis=1), values)
        return carry

    for i in range(1, 8):
        block = x_v.at[core, yh, (z + 8 - i) % 8, pl.ds(0, XROWS)]
        rcopy(block, block, x_ss.at[0], x_rs.at[(z + 8 - i) % 8], dp=twin).wait_recv()
    x_half = x_v.at[core, yh, :, pl.ds(0, XROWS)]
    start(rcopy(x_half, x_half, x_ss.at[8], x_rs.at[8], dp=y_part))

    ag_wait(1, 7, cz_v.at[left_o])
    ag(1, 9, cz_v.at[left_o, 0], right)
    ag_wait(1, 8, cz_v.at[right_o])
    ag(1, 10, cz_v.at[right_o, 1], left)
    wl_make(1)
    wl_make(2)
    ws_make(opp)
    ag_opp_o(1, cz_v)
    wl_make(0)
    settle()
    lax.fori_loop(0, 4, a_add, 0)

    other = x_v.at[core, 1 - yh, :, pl.ds(0, XROWS)]
    rcopy(other, other, x_ss.at[8], x_rs.at[8], dp=y_part).wait_recv()
    x_all = x_v.at[core, :, :, pl.ds(0, XROWS)]
    start(rcopy(x_all, x_all, x_ss.at[9], x_rs.at[9], dp=twin))

    lax.fori_loop(4, 8, a_add, 0)

    base = (me_d * ROWS_DEV).astype(F32)
    live = lax.broadcasted_iota(jnp.int32, (1, 128), 1) < 66

    def x_add(cc):
        def body(i, carry):
            half, first = i // 2, (i % 2) * 4
            hots = []
            for q in range(4):
                low = x_v[cc, half, first + q, 66:67, :].astype(F32)
                high = x_v[cc, half, first + q, 67:68, :].astype(F32)
                ids = jnp.where(live, low + 128 * high - base, -1.0)
                hots.append(jnp.where(row_id == ids, 1.0, 0.0).astype(BF))
            values = x_v[cc, half, pl.ds(pl.multiple_of(first, 4), 4)].reshape(512, 128)
            tg_ref[...] += dot(jnp.concatenate(hots, axis=1), values)
            return carry

        lax.fori_loop(0, 4, body, 0)

    x_add(core)
    x_twin = x_v.at[1 - core, :, :, pl.ds(0, XROWS)]
    rcopy(x_twin, x_twin, x_ss.at[9], x_rs.at[9], dp=twin).wait_recv()
    x_add(1 - core)

    def drain(i, carry):
        a_copy((me_d + i) % DP).wait_send()
        return carry

    lax.fori_loop(1, DP, drain, 0)

    def from_line(half, source, block, arrived):
        @pl.when((unit * 2 + half) * 4 + source != me_d)
        def _():
            rcopy(block, block, ws_ss.at[0], arrived, dp=twin).wait_recv()

    @pl.when(late_here)
    def _():
        for half in range(2):
            total = None
            for source in range(4):
                from_line(half, source, wl_r.at[half, source], wl_rs.at[half, source])
                term = wl_r[half, source].astype(F32)
                total = term if total is None else total + term
            wg_ref[:, half * 128:(half + 1) * 128] = total.astype(BF)

    @pl.when(jnp.logical_not(late_here))
    def _():
        for half in range(2):
            for source in range(4):
                from_line(half, source, ws_r.at[half, source], ws_rs.at[half, source])
                rows = min(64, 2 * PAIRS - source * 64)
                wg_ref[source * 64:source * 64 + rows, half * 128:(half + 1) * 128] = ws_r[half, source, :rows]

    settle()
    for j in (me_s, over, left, right, opp):
        @pl.when(j * 4 + z // 2 != me_d)
        def _():
            ws_copy(j).wait_send()
    for t in range(3):
        @pl.when(late[t] * 4 + z // 2 != me_d)
        def _():
            wl_copy(t).wait_send()


def hand_over(wg_in, tg_in, wg_out, tg_out):
    wg_out[...] = wg_in[...]
    tg_out[...] = tg_in[...]


def on_device(embeddings, cotangent, first_weight, feature_rows):
    vmem = pl.BlockSpec(memory_space=pltpu.VMEM)
    hbm = pl.BlockSpec(memory_space=pl.ANY)
    dma = pltpu.SemaphoreType.DMA
    consts = [jnp.asarray(a) for a in constants()]
    shapes = (jax.ShapeDtypeStruct((2 * PAIRS, 256), BF), jax.ShapeDtypeStruct((ROWS_DEV, 128), F32))
    results = pl.pallas_call(
        kernel,
        out_shape=(pltpu.VMEM((2 * PAIRS, 256), BF), pltpu.VMEM((ROWS_DEV, 128), F32)),
        in_specs=[hbm, hbm, hbm, vmem, hbm, hbm, hbm],
        out_specs=(vmem, vmem),
        scratch_shapes=[
            pltpu.VMEM((2, B, 1024), BF),
            pltpu.VMEM((256, 256), BF),
            pltpu.VMEM((256, 128), BF),
            pltpu.VMEM((256, 256), BF),
            pltpu.VMEM((8, 2, 2, B, 256), BF),
            pltpu.VMEM((8, 2, 4, B, 128), BF),
            pltpu.VMEM((2 * PAIRS, 8192), BF),
            pltpu.VMEM((F, B, 128), BF),
            pltpu.VMEM((F, B, 128), BF),
            pltpu.VMEM((B, 256), F32),
            pltpu.VMEM((2 * PAIRS, 8 * B), BF),
            pltpu.VMEM((B, 256), F32),
            pltpu.VMEM((F, 128), jnp.int32),
            pltpu.VMEM((16, B * F), F32),
            pltpu.VMEM((8, 8, 128), F32),
            pltpu.VMEM((8, 256, B * F), BF),
            pltpu.VMEM((XROWS, B * F), BF),
            pltpu.VMEM((8, 256, 128), F32),
            pltpu.VMEM((8, 256, 128), BF),
            pltpu.VMEM((8, 4, 64, 128), BF),
            pltpu.VMEM((8, 64, 128), BF),
            pltpu.VMEM((2, 4, 64, 128), BF),
            pltpu.VMEM((3, 2 * PAIRS, 128), BF),
            pltpu.VMEM((2, 4, 2 * PAIRS, 128), BF),
            pltpu.VMEM((DP, 64, 128), BF),
            pltpu.VMEM((DP, 64, 128), BF),
            pltpu.VMEM((2, 2, 8, 128, 128), BF),
            dma((10,)), dma((2, 11)), dma((2, 11)), dma((8,)), dma((8,)), dma((8,)), dma((8,)),
            dma((8, 4)), dma((8, 4)), dma((8,)), dma((2, 4)), dma((3,)), dma((2, 4)),
            dma((DP,)), dma((DP,)), dma((10,)), dma((10,)),
        ],
        compiler_params=pltpu.CompilerParams(
            collective_id=0, has_side_effects=True, vmem_limit_bytes=56 * 1024 * 1024),
    )(embeddings, cotangent, first_weight, feature_rows.T, *consts)
    return pl.pallas_call(
        hand_over,
        out_shape=shapes,
        in_specs=[vmem, vmem],
        out_specs=(vmem, vmem),
    )(*[pltpu.with_memory_space_constraint(r, pltpu.VMEM) for r in results])


def solution(mesh):
    return jax.shard_map(
        on_device,
        mesh=mesh,
        in_specs=(P("set", "dp", None), P("dp", "set"), P("set", None), P("dp", None)),
        out_specs=(P("set", "dp"), P("dp", "set")),
        check_vma=False,
    )
```
